256 devices in a mesh: row: 32 (over x, z), col: 8 (over y, core).
Axes of the slice: x: 4, y: 4, z: 8, core: 2. Of those that a mesh axis runs over, the one named last changes fastest.
Arguments:
- tokens: bfloat16 [4096, 5376], P('row', 'col'), may hold values from -6 to 6
- w_query: bfloat16 [5376, 4096], P('row', 'col'), may hold values from -0.078125 to 0.078125
- w_key: bfloat16 [5376, 2048], P('row', 'col'), may hold values from -0.078125 to 0.078125
- w_value: bfloat16 [5376, 2048], P('row', 'col'), may hold values from -0.078125 to 0.078125
- w_output: bfloat16 [4096, 5376], P('col', 'row'), may hold values from -0.09375 to 0.09375
- query_gain: float32 [128], replicated, may hold values from 0.1 to 1.9
- key_gain: float32 [128], replicated, may hold values from 0.1 to 1.9
- cotangent: bfloat16 [4096, 5376], P('row', 'col'), may hold values from -6 to 6
Outputs:
- layer_out: bfloat16 [4096, 5376], P('row', 'col')
- input_grad: bfloat16 [4096, 5376], P('row', 'col')
- grad_query: bfloat16 [5376, 4096], P('row', 'col')
- grad_key: bfloat16 [5376, 2048], P('row', 'col')
- grad_value: bfloat16 [5376, 2048], P('row', 'col')
- grad_output: bfloat16 [4096, 5376], P('col', 'row')
The draws below stay inside these ranges and needn't reach their ends.
All inputs are finite; a program needn't handle non-finite values.
Results may differ from the reference program's by a relative error of at most 0.029.
Values may be sent and summed in bfloat16 or wider, within the bound.
A program may use at most 128 MiB of HBM per device.

```python
import jax
import jax.numpy as jnp
from jax import lax

D = 5376
QH = 32
KVH = 16
HD = 128
WINDOW = 1024
TOK_DEV = 128
TOKENS = 4096
N_ROW = 32


def strengthened(array, own_key, source, target, shards_of, factor):
    def block_of(axis_at):
        return (jnp.arange(array.shape[axis_at]) // (array.shape[axis_at] // shards_of)).reshape((-1,) + (1,) * (array.ndim - 1 - axis_at))

    first = jax.random.permutation(own_key, shards_of)[block_of(target)]
    other_side = (block_of(target) + shards_of // 2) % shards_of
    return jnp.where((block_of(source) == first) | (block_of(source) == other_side), factor * array, array)


def levels(key, extent, pieces, low, top_value):
    gain, own = 1.0, jax.random.fold_in(key, 6)
    for axis_at, parts in pieces:
        draws = jnp.exp(jax.random.uniform(jax.random.fold_in(own, axis_at), (parts,), jnp.float32, low / len(pieces), top_value / len(pieces)))
        gain = gain * jnp.repeat(draws, extent[axis_at] // parts).reshape([-1 if axis == axis_at else 1 for axis in range(len(extent))])
    return gain


def centred(key, dims, deviation, limit, pieces=(), kind=jnp.bfloat16):
    drawn = jax.random.normal(key, dims, jnp.float32) * deviation
    if len(pieces) > 0:
        drawn = levels(key, dims, pieces, -0.22, 0.18) * drawn
    return jnp.clip(drawn, min=-limit, max=limit).astype(kind)


def bell_draw_with(rng, shape, scale, reach, shards, heavy, held_as=jnp.bfloat16):
    array = scale * jax.random.normal(rng, shape, jnp.float32)
    if shards:
        array = array * levels(rng, shape, shards, -0.22, 0.18)
    return jnp.clip(strengthened(array, jax.random.fold_in(rng, 3), *heavy), -reach, reach).astype(held_as)


def setup_inputs(seed: int = 0) -> dict:
    key_of = jax.random.split(jax.random.key(seed), 9)
    return {
        "tokens": bell_draw_with(key_of[0], (TOKENS, D), 1.0, 6.0, ((0, 32), (1, 8)), (0, 1, 32, 2.75)),
        "w_query": centred(key_of[1], (D, QH * HD), D ** -0.5, 0.078125, ((0, 32), (1, 8))),
        "w_key": centred(key_of[2], (D, KVH * HD), D ** -0.5, 0.078125, ((0, 32), (1, 8))),
        "w_value": centred(key_of[3], (D, KVH * HD), D ** -0.5, 0.078125, ((0, 32), (1, 8))),
        "w_output": centred(key_of[4], (QH * HD, D), (QH * HD) ** -0.5, 0.09375, ((0, 8), (1, 32))),
        "query_gain": jnp.clip(1.0 + 0.18 * jax.random.normal(key_of[5], (HD,), jnp.float32), 0.1, 1.9),
        "key_gain": jnp.clip(1.0 + 0.18 * jax.random.normal(key_of[6], (HD,), jnp.float32), 0.1, 1.9),
        "cotangent": bell_draw_with(key_of[7], (TOKENS, D), 1.0, 6.0, ((0, 32), (1, 8)), (0, 1, 32, 2.75)),
    }


query_scalar = 168.0
epsilon = 1e-06

def rms_scale(values, gain_vector):
    mean_square = lax.optimization_barrier(jnp.mean(values * values, axis=-1, keepdims=True))
    return values * lax.rsqrt(mean_square + epsilon) * gain_vector

def attend(queries, key_rows, value_rows, query_gain, key_gain, row_block, neighbours):
    length = queries.shape[0]
    head_width = query_gain.shape[0]
    groups = key_rows.shape[1] // head_width
    repeats = queries.shape[1] // (groups * head_width)
    key_total = key_rows.shape[0]
    query_heads = rms_scale(queries.reshape(length, groups, repeats, head_width), query_gain) * query_scalar ** (-0.5)
    key_heads = rms_scale(key_rows.reshape(key_total, groups, head_width), key_gain)
    value_heads = value_rows.reshape(key_total, groups, head_width)
    scores = jnp.einsum('qgrd,kgd->grqk', query_heads, key_heads)
    query_index = row_block * length + jnp.arange(length, dtype=jnp.int32)
    key_index = (row_block - neighbours) * length + jnp.arange(key_total, dtype=jnp.int32)
    distance = query_index[:, None] - key_index[None, :]
    allowed = (distance >= 0) & (distance < WINDOW) & (key_index[None, :] >= 0)
    scores = jnp.where(allowed, scores, -1e+30)
    row_max = lax.stop_gradient(lax.optimization_barrier(jnp.max(scores, axis=-1, keepdims=True)))
    exponent = jnp.exp(scores - row_max)
    weights = lax.optimization_barrier((exponent / lax.optimization_barrier(jnp.sum(exponent, axis=-1, keepdims=True))).astype(jnp.bfloat16))
    blended = jnp.einsum('grqk,kgd->qgrd', weights.astype(jnp.float32), value_heads)
    return blended.reshape(length, groups * repeats * head_width)

def attention_all(queries, key_rows, value_rows, query_gain, key_gain):
    neighbours = WINDOW // TOK_DEV
    padding = jnp.zeros((neighbours * TOK_DEV, key_rows.shape[1]), jnp.float32)
    key_padded = jnp.concatenate([padding, key_rows], axis=0)
    value_padded = jnp.concatenate([padding, value_rows], axis=0)

    def one_block(row_block):
        offset = (row_block * TOK_DEV).astype(jnp.int32)
        block_queries = lax.dynamic_slice_in_dim(queries, offset, TOK_DEV, 0)
        block_keys = lax.dynamic_slice_in_dim(key_padded, offset, (neighbours + 1) * TOK_DEV, 0)
        block_values = lax.dynamic_slice_in_dim(value_padded, offset, (neighbours + 1) * TOK_DEV, 0)
        return attend(block_queries, block_keys, block_values, query_gain, key_gain, row_block, neighbours)
    outputs = lax.map(one_block, jnp.arange(TOKENS // TOK_DEV, dtype=jnp.int32))
    return outputs.reshape(TOKENS, queries.shape[1])

def block_sum(left_side, right_side):
    left_blocks = left_side.reshape(N_ROW, TOK_DEV, left_side.shape[1])
    right_blocks = right_side.reshape(N_ROW, TOK_DEV, right_side.shape[1])

    def add_block(running, blocks):
        term = lax.dot_general(blocks[0], blocks[1], (((0,), (0,)), ((), ())), preferred_element_type=jnp.float32)
        rounded = lax.optimization_barrier(term.astype(jnp.bfloat16))
        return (running + rounded.astype(jnp.float32), None)
    initial = jnp.zeros((left_side.shape[1], right_side.shape[1]), jnp.float32)
    summed, unused = lax.scan(add_block, initial, (left_blocks, right_blocks))
    return summed.astype(jnp.bfloat16)

def reference(tokens, w_query, w_key, w_value, w_output, query_gain, key_gain, cotangent):
    queries = jnp.dot(tokens, w_query, preferred_element_type=jnp.float32).astype(jnp.bfloat16)
    key_rows = jnp.dot(tokens, w_key, preferred_element_type=jnp.float32).astype(jnp.bfloat16)
    value_rows = jnp.dot(tokens, w_value, preferred_element_type=jnp.float32).astype(jnp.bfloat16)

    def attention_of(query_in, key_in, value_in):
        return attention_all(query_in, key_in, value_in, query_gain, key_gain)
    blended, pullback = jax.vjp(attention_of, queries.astype(jnp.float32), key_rows.astype(jnp.float32), value_rows.astype(jnp.float32))
    attended = blended.astype(jnp.bfloat16)
    layer_out = jnp.dot(attended, w_output, preferred_element_type=jnp.float32).astype(jnp.bfloat16)
    grad_attended = jnp.dot(cotangent, w_output.T, preferred_element_type=jnp.float32).astype(jnp.bfloat16)
    grad_queries, grad_keys, grad_values = pullback(grad_attended.astype(jnp.float32))
    query_grad_bf = grad_queries.astype(jnp.bfloat16)
    key_grad_bf = grad_keys.astype(jnp.bfloat16)
    value_grad_bf = grad_values.astype(jnp.bfloat16)
    input_sum = jnp.dot(query_grad_bf, w_query.T, preferred_element_type=jnp.float32)
    input_sum = input_sum + jnp.dot(key_grad_bf, w_key.T, preferred_element_type=jnp.float32)
    input_sum = input_sum + jnp.dot(value_grad_bf, w_value.T, preferred_element_type=jnp.float32)
    input_grad = input_sum.astype(jnp.bfloat16)
    grad_query = block_sum(tokens, query_grad_bf)
    grad_key = block_sum(tokens, key_grad_bf)
    grad_value = block_sum(tokens, value_grad_bf)
    grad_output = block_sum(attended, cotangent)
    return (layer_out, input_grad, grad_query, grad_key, grad_value, grad_output)
```

```python
import functools

import jax
import jax.numpy as jnp
from jax import lax
from jax.experimental import pallas as pl
from jax.experimental.pallas import tpu as pltpu
from jax.sharding import PartitionSpec as P

BF16 = jnp.bfloat16
F32 = jnp.float32

NX, NZ, NY = 4, 8, 4

OWN, SENT, PITCH, BLOCK = 168, 176, 192, 768
TOK = 128
SLAB = 2 * TOK
HD = 128
BACK = 4
KEYS = (BACK + 1) * SLAB
WINDOW = 1024
QKV, OUT = 0, 1
WIDTH = (512, 256)
query_scalar = 168.0
epsilon = 1e-06


def dot(a, b, ca, cb):
    return lax.dot_general(a, b, (((ca,), (cb,)), ((), ())), preferred_element_type=F32)


def remainder(a, b):
    return lax.rem(a + b, b)


def near_first(i):
    odd = lax.rem(i, 2)
    return odd * lax.div(i + 1, 2) + (1 - odd) * lax.rem(8 - lax.div(i, 2), 8)


def spread():
    i = lax.broadcasted_iota(jnp.int32, (4 * OWN, BLOCK), 0)
    j = lax.broadcasted_iota(jnp.int32, (4 * OWN, BLOCK), 1)
    group = (
        (i >= OWN).astype(jnp.int32)
        + (i >= 2 * OWN).astype(jnp.int32)
        + (i >= 3 * OWN).astype(jnp.int32)
    )
    return (j == i + (PITCH - OWN) * group).astype(F32).astype(BF16)


def kernel(
    tok_in, cot_in, wq_in, wk_in, wv_in, wo_in, qg_ref, kg_ref,
    layer_out, input_grad, gq_out, gk_out, gv_out, go_out,
    place, tok, cot, pack_qkv, pack_out, w_qkv, w_out, g_qkv, g_out,
    acc, q_raw, qh, kh, kvwin, scores, pb, ds, att, datt, dkv, dkv_own, dkv_in, dqkv,
    ybuf, ysib, yrecv, zbuf, zsib, zrecv,
    relay_qkv, relay_out, full_qkv, full_out, ring_qkv, ring_out,
    s_loc, s_z, r_z, s_xf, r_xf, s_xh, r_xh, s_t, r_t, s_s, r_s, s_kv, r_kv, s_dk, r_dk,
    s_rl, r_rl, s_fl, r_fl, s_rz, r_rz, s_ys, r_ys, s_yy, r_yy,
):
    row = lax.axis_index("row")
    col = lax.axis_index("col")
    x, z = lax.div(row, NZ), lax.rem(row, NZ)
    y, core = lax.div(col, 2), lax.rem(col, 2)
    par = lax.rem(z, 2)
    pair = lax.div(row, 2)
    xs = [x, lax.rem(x + 1, NX), lax.rem(x + 2, NX), lax.rem(x + 3, NX)]
    sibling = col + 1 - 2 * core

    def remote(src, dst, ssem, rsem, to_row, to_col):
        return pltpu.make_async_remote_copy(
            src_ref=src, dst_ref=dst, send_sem=ssem, recv_sem=rsem,
            device_id={"row": to_row, "col": to_col}, device_id_type=pl.DeviceIdType.MESH,
        )

    def ring_row(d):
        return x * NZ + lax.rem(z + d, NZ)

    def group_at(e, sign):
        dy, dq = lax.div(e, 2), lax.rem(e, 2)
        yt = lax.rem(y + NY + sign * dy, NY)
        return row + dq * (1 - 2 * par), yt * 2 + core

    def back_row(i):
        return 2 * lax.rem(pair + 16 - i, 16) + par

    barrier = pltpu.get_barrier_semaphore()

    def greet(to_row, to_col):
        pl.semaphore_signal(
            barrier, inc=1, device_id={"row": to_row, "col": to_col},
            device_id_type=pl.DeviceIdType.MESH,
        )

    @pl.loop(1, 8)
    def _(d):
        greet(ring_row(d), col)
        gr, gc = group_at(d, 1)
        greet(gr, gc)

    @pl.loop(1, BACK + 1)
    def _(i):
        greet(back_row(i), col)
        greet(back_row(16 - i), col)

    greet(row, sibling)
    greet(xs[1] * NZ + z, col)
    greet(xs[3] * NZ + z, col)

    packs = (pack_qkv, pack_out)
    fulls_w = (w_qkv, w_out)
    grads = (g_qkv, g_out)

    def rows_of(xx, zz):
        return 2 * xx + lax.div(zz, 4), pl.ds(pl.multiple_of(PITCH * lax.rem(zz, 4), 16), SENT)

    def block(ref, xx, zz):
        c, rows = rows_of(xx, zz)
        return ref.at[c, rows]

    def half_of(a, side):
        return pl.ds(side * (WIDTH[a] // 2), WIDTH[a] // 2)

    def half(ref, a, xx, zz, side):
        c, rows = rows_of(xx, zz)
        return ref.at[c, rows, half_of(a, side)]

    for q in (0, 1):
        pack_qkv[q, 160:SENT, :] = jnp.zeros((16, 512), BF16)
        pack_qkv[q, 0:OWN, 0:256] = wq_in[:, 256 * q : 256 * q + 256]
        pack_qkv[q, 0:OWN, 256:384] = wk_in[:, 128 * q : 128 * q + 128]
        pack_qkv[q, 0:OWN, 384:512] = wv_in[:, 128 * q : 128 * q + 128]
        pack_out[q, 160:SENT, :] = jnp.zeros((16, 256), BF16)
        pack_out[q, 0:OWN, :] = wo_in[:, 256 * q : 256 * q + 256]

    pl.semaphore_wait(barrier, 25)

    def z_copy(a, d, zs, zt):
        return remote(
            packs[a].at[lax.rem(zt, 2)], block(fulls_w[a], x, zs),
            s_z.at[a, d], r_z.at[a, d], x * NZ + zt, col,
        )

    def z_start(a):
        pltpu.make_async_copy(packs[a].at[par], block(fulls_w[a], x, z), s_loc.at[a]).start()

        @pl.loop(1, 8)
        def _(i):
            d = near_first(i)
            z_copy(a, d, z, lax.rem(z + d, NZ)).start()

    z_start(QKV)

    place[...] = spread()
    own_rows = pl.ds(pl.multiple_of(TOK * par, TOK), TOK)

    def t_slot(ref, e, cc):
        dy, dq = lax.div(e, 2), lax.rem(e, 2)
        c = lax.rem(y + NY - dy, NY) * 2 + cc
        q = par + dq * (1 - 2 * par)
        return ref.at[c, pl.ds(pl.multiple_of(TOK * q, TOK), TOK)]

    slabs = (tok, cot)

    def t_copy(t, e):
        gr, gc = group_at(e, 1)
        own = slabs[t].at[col, own_rows]
        return remote(own, own, s_t.at[t, e], r_t.at[t, e], gr, gc)

    def t_recv(t, e):
        gr, gc = group_at(e, 1)
        slot = t_slot(slabs[t], e, core)
        return remote(slot, slot, s_t.at[t, e], r_t.at[t, e], gr, gc)

    def sib_copy(t, e, cc):
        slot = t_slot(slabs[t], e, cc)
        return remote(slot, slot, s_s.at[t, e], r_s.at[t, e], row, sibling)

    for t, src in ((0, tok_in), (1, cot_in)):
        slabs[t][col, own_rows] = dot(src[...], place[...], 1, 0).astype(BF16)

        @pl.loop(1, 8)
        def _(e):
            t_copy(t, e).start()

        sib_copy(t, 0, core).start()

    for c in range(8):
        for j in range(4):
            gap = slice(PITCH * j + SENT, PITCH * (j + 1))
            w_qkv[c, gap, :] = jnp.zeros((PITCH - SENT, 512), BF16)
            w_out[c, gap, :] = jnp.zeros((PITCH - SENT, 256), BF16)

    def xf_copy(a, i, side, xx):
        slot = block(fulls_w[a], xx, remainder(z - near_first(i), NZ))
        to = xs[1] if side == 0 else xs[3]
        return remote(slot, slot, s_xf.at[a, side, i], r_xf.at[a, side, i], to * NZ + z, col)

    def xh_copy(a, i, side, xx):
        slot = half(fulls_w[a], a, xx, remainder(z - near_first(i), NZ), side)
        to = xs[1] if side == 0 else xs[3]
        return remote(slot, slot, s_xh.at[a, side, i], r_xh.at[a, side, i], to * NZ + z, col)

    def gather_first(a, i, own):
        if own:
            pltpu.make_async_copy(packs[a].at[par], block(fulls_w[a], x, z), s_loc.at[a]).wait()
        else:
            d = near_first(i)
            z_copy(a, d, remainder(z - d, NZ), z).wait_recv()
        xf_copy(a, i, 0, x).start()
        xf_copy(a, i, 1, x).start()

    def gather_second(a, i):
        xf_copy(a, i, 0, xs[3]).wait_recv()
        xh_copy(a, i, 0, xs[3]).start()
        xf_copy(a, i, 1, xs[1]).wait_recv()
        xh_copy(a, i, 1, xs[1]).start()

    def gather_third(a, i):
        xh_copy(a, i, 0, xs[2]).wait_recv()
        xh_copy(a, i, 1, xs[2]).wait_recv()

    def share(t):
        @pl.loop(1, 8)
        def _(e):
            t_recv(t, e).wait_recv()
            sib_copy(t, e, core).start()

    def shared(t):
        @pl.loop(0, 8)
        def _(e):
            sib_copy(t, e, 1 - core).wait_recv()

    zero = jnp.int32(0)
    gather_first(QKV, zero, True)

    @pl.loop(1, 8)
    def _(i):
        gather_first(QKV, i, False)
        gather_second(QKV, i - 1)

    z_start(OUT)
    gather_second(QKV, jnp.int32(7))
    share(0)
    shared(0)

    acc[...] = jnp.zeros_like(acc)

    def project(xx):
        @pl.loop(0, 2)
        def _(cc):
            c = 2 * xx + cc
            acc[...] += dot(tok[c], w_qkv[c], 1, 0)

    project(xs[0])
    project(xs[1])
    project(xs[3])

    gather_first(OUT, zero, True)

    @pl.loop(1, 8)
    def _(i):
        gather_first(OUT, i, False)

    @pl.loop(0, 8)
    def _(i):
        gather_third(QKV, i)

    project(xs[2])

    own_keys = pl.ds(BACK * SLAB, SLAB)
    kvwin[own_keys, :] = acc[:, 256:512].astype(BF16)

    def kv_copy(i):
        return remote(
            kvwin.at[own_keys], kvwin.at[pl.ds((BACK - i) * SLAB, SLAB)],
            s_kv.at[i - 1], r_kv.at[i - 1], back_row(16 - i), col,
        )

    for i in range(1, BACK + 1):
        kv_copy(i).start()

    def scale_of(values):
        return lax.rsqrt(jnp.mean(values * values, axis=-1, keepdims=True) + epsilon)

    qgain = qg_ref[...] * query_scalar ** (-0.5)
    kgain = kg_ref[...]
    for h in range(2):
        lanes = slice(HD * h, HD * h + HD)
        q = acc[:, lanes].astype(BF16)
        q_raw[:, lanes] = q
        q = q.astype(F32)
        qh[SLAB * h : SLAB * h + SLAB, :] = (q * scale_of(q) * qgain).astype(BF16)

    share(1)

    @pl.loop(0, 8)
    def _(i):
        gather_second(OUT, i)

    for i in range(1, BACK + 1):
        kv_copy(i).wait_recv()

    @pl.loop(0, BACK + 1)
    def _(s):
        rows = pl.ds(pl.multiple_of(s * SLAB, SLAB), SLAB)
        k = kvwin[rows, 0:HD].astype(F32)
        kh[rows, :] = (k * scale_of(k) * kgain).astype(BF16)

    scores[...] = dot(qh[...], kh[...], 1, 1)
    chunk = 32
    first_key = WINDOW - SLAB * pair

    @pl.loop(0, 2 * SLAB // chunk)
    def _(n):
        rows = pl.ds(pl.multiple_of(n * chunk, chunk), chunk)
        t0 = lax.rem(n, SLAB // chunk) * chunk
        t = t0 + lax.broadcasted_iota(jnp.int32, (chunk, 1), 0)
        key = lax.broadcasted_iota(jnp.int32, (chunk, KEYS), 1)
        allowed = (key <= t + WINDOW) & (key >= jnp.maximum(t + 1, first_key))
        s = jnp.where(allowed, scores[rows, :], -1e30)
        e = jnp.exp(s - jnp.max(s, axis=-1, keepdims=True))
        pb[rows, :] = (e * (1.0 / jnp.sum(e, axis=-1, keepdims=True))).astype(BF16)

    blended = dot(pb[...], kvwin[:, HD:], 1, 0).astype(BF16)
    att[:, 0:HD] = blended[0:SLAB]
    att[:, HD:] = blended[SLAB:]

    shared(1)

    relays = (relay_qkv, relay_out)
    fulls = (full_qkv, full_out)
    rings = (ring_qkv, ring_out)

    def rl_copy(a, zz, side):
        to = xs[1] if side == 0 else xs[3]
        return remote(
            half(grads[a], a, xs[2], zz, side), relays[a].at[side, zz],
            s_rl.at[a, side, zz], r_rl.at[a, side, zz], to * NZ + z, col,
        )

    def fl_copy(a, zz, side):
        to = xs[1] if side == 0 else xs[3]
        return remote(
            block(grads[a], to, zz), fulls[a].at[side, zz],
            s_fl.at[a, side, zz], r_fl.at[a, side, zz], to * NZ + z, col,
        )

    def rz_copy(a, d, slot):
        zt = lax.rem(z + d, NZ)
        return remote(
            block(grads[a], x, zt), rings[a].at[slot],
            s_rz.at[a, d], r_rz.at[a, d], x * NZ + zt, col,
        )

    def far_first(i):
        return lax.rem(z + near_first(7 - i), NZ)

    def reduce_start(a):
        @pl.loop(0, 8)
        def _(i):
            rl_copy(a, far_first(i), 0).start()
            rl_copy(a, far_first(i), 1).start()

    def reduce_second(a, i):
        zz = far_first(i)
        for side in (0, 1):
            rl_copy(a, zz, side).wait_recv()
            to = xs[1] if side == 0 else xs[3]
            c, rows = rows_of(to, zz)
            lanes = half_of(a, side)
            grads[a][c, rows, lanes] = (
                grads[a][c, rows, lanes].astype(F32) + relays[a][side, zz].astype(F32)
            ).astype(BF16)
            fl_copy(a, zz, side).start()

    def reduce_third(a, i, own):
        zz = far_first(i)
        fl_copy(a, zz, 0).wait_recv()
        fl_copy(a, zz, 1).wait_recv()
        c, rows = rows_of(x, zz)
        total = (
            grads[a][c, rows, :].astype(F32)
            + fulls[a][0, zz].astype(F32)
            + fulls[a][1, zz].astype(F32)
        ).astype(BF16)
        if own:
            rings[a][z] = total
        else:
            grads[a][c, rows, :] = total
            rz_copy(a, near_first(7 - i), z).start()

    def reduce_last(a, q):
        total = rings[a][q].astype(F32)
        for k in (2, 4, 6):
            total = total + rings[a][q + k].astype(F32)
        return total.astype(BF16)

    def reduce_middle(a):
        reduce_second(a, zero)

        @pl.loop(1, 8)
        def _(i):
            reduce_second(a, i)
            reduce_third(a, i - 1, False)

        reduce_third(a, jnp.int32(7), True)

    def reduce_wait(a):
        @pl.loop(1, 8)
        def _(d):
            rz_copy(a, d, remainder(z - d, NZ)).wait_recv()

    ybufs, ysibs, yrecvs = (ybuf, zbuf), (ysib, zsib), (yrecv, zrecv)

    def ys_copy(t, yy):
        return remote(
            ybufs[t].at[2 * yy + 1 - core], ysibs[t].at[yy],
            s_ys.at[t, yy], r_ys.at[t, yy], row, sibling,
        )

    def yy_copy(t, e):
        gr, gc = group_at(e, 1)
        q = par + lax.rem(e, 2) * (1 - 2 * par)
        return remote(
            ybufs[t].at[gc, pl.ds(pl.multiple_of(TOK * q, TOK), TOK)], yrecvs[t].at[e],
            s_yy.at[t, e], r_yy.at[t, e], gr, gc,
        )

    def sum_start(t):
        @pl.loop(0, NY)
        def _(yy):
            ys_copy(t, yy).start()

    def sum_second(t):
        @pl.loop(0, NY)
        def _(i):
            dy = lax.rem(i + 2, NY)
            yy = lax.rem(y + dy, NY)
            ys_copy(t, yy).wait_recv()
            c = 2 * yy + core
            ybufs[t][c] = (ybufs[t][c].astype(F32) + ysibs[t][yy].astype(F32)).astype(BF16)

            @pl.when(i != 2)
            def _():
                yy_copy(t, 2 * dy).start()

            yy_copy(t, 2 * dy + 1).start()

    def sum_last(t, out):
        @pl.loop(1, 8)
        def _(e):
            yy_copy(t, e).wait_recv()

        total = ybufs[t][col, own_rows].astype(F32)
        for e in range(1, 8):
            total = total + yrecvs[t][e].astype(F32)
        out[...] = dot(total.astype(BF16), place[...], 1, 1).astype(BF16)

    for k in (2, 1, 3, 0):
        @pl.loop(0, 2)
        def _(cc):
            c = 2 * xs[k] + cc
            g_out[c] = dot(cot[c], att[...], 0, 0).astype(BF16)

        if k == 2:
            reduce_start(OUT)

    @pl.loop(0, 8)
    def _(i):
        gather_third(OUT, i)

    acc[:, 0:256] = jnp.zeros((SLAB, 256), F32)

    @pl.loop(0, 8)
    def _(c):
        acc[:, 0:256] += dot(cot[c], w_out[c], 1, 0)
        ybuf[c] = dot(att[...], w_out[c], 1, 1).astype(BF16)

    sum_start(0)
    for h in range(2):
        datt[SLAB * h : SLAB * h + SLAB, :] = acc[:, HD * h : HD * h + HD].astype(BF16)

    scores[...] = dot(datt[...], kvwin[:, HD:], 1, 1)

    @pl.loop(0, 2 * SLAB // chunk)
    def _(n):
        rows = pl.ds(pl.multiple_of(n * chunk, chunk), chunk)
        p = pb[rows, :].astype(F32)
        dp = scores[rows, :]
        delta = jnp.sum(p * dp, axis=-1, keepdims=True)
        ds[rows, :] = (p * (dp - delta)).astype(BF16)

    def norm_back(raw, gain, grad):
        r = scale_of(raw)
        inner = grad * gain
        return r * inner - raw * (r * r * r * jnp.mean(raw * inner, axis=-1, keepdims=True))

    dkh = dot(ds[...], qh[...], 0, 0)
    dvh = dot(pb[...], datt[...], 0, 0)
    for s in range(BACK + 1):
        rows = slice(s * SLAB, s * SLAB + SLAB)
        dk = norm_back(kvwin[rows, 0:HD].astype(F32), kgain, dkh[rows])
        if s == BACK:
            dkv_own[:, 0:HD] = dk
            dkv_own[:, HD:] = dvh[rows]
        else:
            dkv[s, :, 0:HD] = dk.astype(BF16)
            dkv[s, :, HD:] = dvh[rows].astype(BF16)

    def dk_copy(i):
        return remote(
            dkv.at[BACK - i], dkv_in.at[i - 1], s_dk.at[i - 1], r_dk.at[i - 1], back_row(i), col,
        )

    for i in range(1, BACK + 1):
        dk_copy(i).start()

    dqh = dot(ds[...], kh[...], 1, 0)
    for h in range(2):
        lanes = slice(HD * h, HD * h + HD)
        dqkv[:, lanes] = norm_back(
            q_raw[:, lanes].astype(F32), qgain, dqh[SLAB * h : SLAB * h + SLAB]
        ).astype(BF16)

    sum_second(0)
    reduce_middle(OUT)

    for i in range(1, BACK + 1):
        dk_copy(i).wait_recv()
    total = dkv_own[...]
    for i in range(BACK):
        total = total + dkv_in[i].astype(F32)
    dqkv[:, 256:512] = total.astype(BF16)

    for k in (2, 1, 3, 0):
        @pl.loop(0, 2)
        def _(cc):
            c = 2 * xs[k] + cc
            g_qkv[c] = dot(tok[c], dqkv[...], 0, 0).astype(BF16)

        if k == 2:
            reduce_start(QKV)

    @pl.loop(0, 8)
    def _(c):
        zbuf[c] = dot(dqkv[...], w_qkv[c], 1, 1).astype(BF16)

    sum_start(1)
    sum_second(1)
    reduce_middle(QKV)

    sum_last(0, layer_out)
    reduce_wait(OUT)
    for q in (0, 1):
        go_out[:, 256 * q : 256 * q + 256] = reduce_last(OUT, q)[0:OWN]
    sum_last(1, input_grad)
    reduce_wait(QKV)
    for q in (0, 1):
        done = reduce_last(QKV, q)
        gq_out[:, 256 * q : 256 * q + 256] = done[0:OWN, 0:256]
        gk_out[:, 128 * q : 128 * q + 128] = done[0:OWN, 256:384]
        gv_out[:, 128 * q : 128 * q + 128] = done[0:OWN, 384:512]

    for a in (QKV, OUT):
        @pl.loop(1, 8)
        def _(d):
            z_copy(a, d, z, lax.rem(z + d, NZ)).wait_send()
            rz_copy(a, d, z).wait_send()

        @pl.loop(0, 8)
        def _(i):
            for side in (0, 1):
                xf_copy(a, i, side, x).wait_send()
                xh_copy(a, i, side, xs[3] if side == 0 else xs[1]).wait_send()
                rl_copy(a, i, side).wait_send()
                fl_copy(a, i, side).wait_send()

    for t in (0, 1):
        @pl.loop(1, 8)
        def _(e):
            t_copy(t, e).wait_send()
            yy_copy(t, e).wait_send()

        @pl.loop(0, 8)
        def _(e):
            sib_copy(t, e, core).wait_send()

        @pl.loop(0, NY)
        def _(yy):
            ys_copy(t, yy).wait_send()

    for i in range(1, BACK + 1):
        kv_copy(i).wait_send()
        dk_copy(i).wait_send()


def shards(tokens, w_query, w_key, w_value, w_output, query_gain, key_gain, cotangent):
    vmem = lambda *shape, dtype=BF16: pltpu.VMEM(shape, dtype)
    dma = lambda *shape: pltpu.SemaphoreType.DMA(shape)
    spec = pl.BlockSpec(memory_space=pltpu.VMEM)
    scratch = [
        vmem(4 * OWN, BLOCK),
        vmem(8, SLAB, BLOCK), vmem(8, SLAB, BLOCK),
        vmem(2, SENT, 512), vmem(2, SENT, 256),
        vmem(8, BLOCK, 512), vmem(8, BLOCK, 256),
        vmem(8, BLOCK, 512), vmem(8, BLOCK, 256),
        vmem(SLAB, 512, dtype=F32), vmem(SLAB, 256), vmem(2 * SLAB, HD), vmem(KEYS, HD),
        vmem(KEYS, 2 * HD), vmem(2 * SLAB, KEYS, dtype=F32), vmem(2 * SLAB, KEYS),
        vmem(2 * SLAB, KEYS), vmem(SLAB, 256), vmem(2 * SLAB, HD),
        vmem(BACK, SLAB, 256), vmem(SLAB, 256, dtype=F32), vmem(BACK, SLAB, 256), vmem(SLAB, 512),
        vmem(8, SLAB, BLOCK), vmem(NY, SLAB, BLOCK), vmem(8, TOK, BLOCK),
        vmem(8, SLAB, BLOCK), vmem(NY, SLAB, BLOCK), vmem(8, TOK, BLOCK),
        vmem(2, 8, SENT, 256), vmem(2, 8, SENT, 128),
        vmem(2, 8, SENT, 512), vmem(2, 8, SENT, 256),
        vmem(8, SENT, 512), vmem(8, SENT, 256),
        dma(2),
        dma(2, 8), dma(2, 8),
        dma(2, 2, 8), dma(2, 2, 8),
        dma(2, 2, 8), dma(2, 2, 8),
        dma(2, 8), dma(2, 8),
        dma(2, 8), dma(2, 8),
        dma(BACK), dma(BACK), dma(BACK), dma(BACK),
        dma(2, 2, 8), dma(2, 2, 8),
        dma(2, 2, 8), dma(2, 2, 8),
        dma(2, 8), dma(2, 8),
        dma(2, NY), dma(2, NY),
        dma(2, 8), dma(2, 8),
    ]
    outs = [
        jax.ShapeDtypeStruct(tokens.shape, BF16),
        jax.ShapeDtypeStruct(tokens.shape, BF16),
        jax.ShapeDtypeStruct(w_query.shape, BF16),
        jax.ShapeDtypeStruct(w_key.shape, BF16),
        jax.ShapeDtypeStruct(w_value.shape, BF16),
        jax.ShapeDtypeStruct(w_output.shape[::-1], BF16),
    ]
    layer_out, input_grad, gq, gk, gv, go = pl.pallas_call(
        kernel,
        out_shape=outs,
        in_specs=[spec] * 8,
        out_specs=[spec] * 6,
        scratch_shapes=scratch,
        compiler_params=pltpu.CompilerParams(
            collective_id=0, has_side_effects=True, vmem_limit_bytes=64 * 1024 * 1024 - 65536
        ),
    )(
        tokens, cotangent, w_query, w_key, w_value, w_output.T,
        query_gain.reshape(1, HD), key_gain.reshape(1, HD),
    )
    return layer_out, input_grad, gq, gk, gv, go.T


def solution(mesh):
    in_specs = (
        P("row", "col"), P("row", "col"), P("row", "col"), P("row", "col"), P("col", "row"),
        P(), P(), P("row", "col"),
    )
    out_specs = (
        P("row", "col"), P("row", "col"), P("row", "col"), P("row", "col"), P("row", "col"),
        P("col", "row"),
    )
    return jax.shard_map(shards, mesh=mesh, in_specs=in_specs, out_specs=out_specs, check_vma=False)
```

```python
import jax
import jax.numpy as jnp
from jax import lax
from jax.experimental import pallas as pl
from jax.experimental.pallas import tpu as pltpu
from jax.sharding import PartitionSpec as P

BF16 = jnp.bfloat16
F32 = jnp.float32

NX, NZ, NY = 4, 8, 4

OWN, SENT, PITCH, BLOCK = 168, 176, 192, 768
TOK = 128
SUPER = 1024
SLAB = 256
HD = 128
BACK = 4
KEYS = (BACK + 1) * SLAB
WINDOW = 1024
KV, Q, OUT = 0, 1, 2
ATT, DQ, DKV = 0, 1, 2
query_scalar = 168.0
epsilon = 1e-06


def dot(a, b, ca, cb):
    return lax.dot_general(a, b, (((ca,), (cb,)), ((), ())), preferred_element_type=F32)


def ring(a, n):
    return lax.rem(a + n, n)


def spread():
    i = lax.broadcasted_iota(jnp.int32, (4 * OWN, BLOCK), 0)
    j = lax.broadcasted_iota(jnp.int32, (4 * OWN, BLOCK), 1)
    group = (
        (i >= OWN).astype(jnp.int32)
        + (i >= 2 * OWN).astype(jnp.int32)
        + (i >= 3 * OWN).astype(jnp.int32)
    )
    return (j == i + (PITCH - OWN) * group).astype(F32).astype(BF16)


def kernel(
    tok_in, cot_in, wq_in, wk_in, wv_in, wo_in, qg_ref, kg_ref,
    layer_out, input_grad, gq_out, gk_out, gv_out, go_out,
    place, piece, slabs, w, g, part, sum_half, sum_full, gath,
    q_raw, qh, kh, kvwin, scores, pb, ds, datt, dkv, dkv_own, dkv_in,
    ypart, ysib, yrecv, last, relay, full,
    s_xf, r_xf, s_xh, r_xh, s_p, r_p, s_y, r_y, s_s, r_s, s_l,
    s_rs, r_rs, s_ag, r_ag, s_ah, r_ah, s_kv, r_kv, s_dk, r_dk,
    s_rl, r_rl, s_fl, r_fl, s_os, r_os, s_oy, r_oy, s_oz, r_oz,
):
    row = lax.axis_index("row")
    col = lax.axis_index("col")
    x, z = lax.div(row, NZ), lax.rem(row, NZ)
    y, core = lax.div(col, 2), lax.rem(col, 2)
    head, quarter = lax.div(z, 4), lax.rem(z, 4)
    collects = core == head
    xs = [ring(x + d, NX) for d in range(NX)]
    zs = [ring(z + d, NZ) for d in range(NZ)]
    ys = [ring(y + d, NY) for d in range(NY)]
    sibling = col + 1 - 2 * core
    place_in_ring = 4 * x + quarter

    def remote(src, dst, ssem, rsem, to_row, to_col):
        return pltpu.make_async_remote_copy(
            src_ref=src, dst_ref=dst, send_sem=ssem, recv_sem=rsem,
            device_id={"row": to_row, "col": to_col}, device_id_type=pl.DeviceIdType.MESH,
        )

    def token_row(i):
        at = lax.rem(place_in_ring + 16 + i, 16)
        return lax.div(at, 4) * NZ + 4 * head + lax.rem(at, 4)

    def x_row(side):
        return (xs[1] if side == 0 else xs[3]) * NZ + z

    def z_row(side):
        return x * NZ + (zs[1] if side == 0 else zs[7])

    barrier = pltpu.get_barrier_semaphore()

    def greet(to_row, to_col):
        pl.semaphore_signal(
            barrier, inc=1, device_id={"row": to_row, "col": to_col},
            device_id_type=pl.DeviceIdType.MESH,
        )

    for d in range(1, NZ):
        greet(x * NZ + zs[d], col)
    for d in range(1, NY):
        greet(row, 2 * ys[d] + core)
    for i in range(1, BACK + 1):
        greet(token_row(i), col)
        greet(token_row(-i), col)
    greet(row, sibling)
    greet(x_row(0), col)
    greet(x_row(1), col)

    def rows_at(i):
        return pl.ds(pl.multiple_of(PITCH * i, 16), SENT)

    own_rows = rows_at(x)
    for u in (KV, Q, OUT):
        w[u, pl.ds(pl.multiple_of(PITCH * x + 160, 16), 16), :] = jnp.zeros((16, 512), BF16)
    weight_rows = pl.ds(pl.multiple_of(PITCH * x, 16), OWN)
    for h in (0, 1):
        w[KV, weight_rows, 256 * h : 256 * h + 128] = wk_in[:, 128 * h : 128 * h + 128]
        w[KV, weight_rows, 256 * h + 128 : 256 * h + 256] = wv_in[:, 128 * h : 128 * h + 128]
    w[Q, weight_rows, :] = wq_in[...]
    w[OUT, weight_rows, :] = wo_in[...]

    pl.semaphore_wait(barrier, 21)

    def xf_copy(u, side, xx):
        slot = w.at[u, rows_at(xx)]
        return remote(slot, slot, s_xf.at[u, side], r_xf.at[u, side], x_row(side), col)

    def xh_copy(u, side, xx):
        slot = w.at[u, rows_at(xx), pl.ds(256 * side, 256)]
        return remote(slot, slot, s_xh.at[u, side], r_xh.at[u, side], x_row(side), col)

    def weight_start(u):
        xf_copy(u, 0, x).start()
        xf_copy(u, 1, x).start()

    def weight_forward(u):
        xf_copy(u, 0, xs[3]).wait_recv()
        xh_copy(u, 0, xs[3]).start()
        xf_copy(u, 1, xs[1]).wait_recv()
        xh_copy(u, 1, xs[1]).start()

    def weight_wait(u):
        xh_copy(u, 0, xs[2]).wait_recv()
        xh_copy(u, 1, xs[2]).wait_recv()

    for u in (KV, Q, OUT):
        weight_start(u)

    def lanes_at(i):
        return pl.ds(pl.multiple_of(TOK * i, TOK), TOK)

    def piece_copy(t, j, zt):
        return remote(
            piece.at[t, pl.ds(pl.multiple_of(PITCH * j, 16), SENT)],
            slabs.at[t, rows_at(y), lanes_at(z)],
            s_p.at[t, j], r_p.at[t, z], x * NZ + zt, col,
        )

    def piece_recv(t, zf):
        slot = slabs.at[t, rows_at(y), lanes_at(zf)]
        return remote(slot, slot, s_p.at[t, 0], r_p.at[t, zf], x * NZ + zf, col)

    def piece_own(t):
        return pltpu.make_async_copy(
            piece.at[t, pl.ds(pl.multiple_of(PITCH * quarter, 16), SENT)],
            slabs.at[t, rows_at(y), lanes_at(z)], s_l.at[t],
        )

    def piece_start(t):
        @pl.loop(0, 4)
        def _(i):
            j = lax.rem(quarter + 1 + i, 4)
            zt = 4 * core + j

            @pl.when(zt != z)
            def _():
                piece_copy(t, j, zt).start()

        @pl.when(collects)
        def _():
            piece_own(t).start()

    def slab_copy(t, dy, yy):
        slot = slabs.at[t, rows_at(yy)]
        return remote(slot, slot, s_y.at[t, dy], r_y.at[t, dy], row, 2 * ys[dy] + core)

    def share_copy(t, dy):
        slot = slabs.at[t, rows_at(ys[(NY - dy) % NY])]
        return remote(slot, slot, s_s.at[t, dy], r_s.at[t, dy], row, sibling)

    def collect(t):
        @pl.when(collects)
        def _():
            piece_own(t).wait()
            for d in range(1, NZ):
                piece_recv(t, zs[d]).wait_recv()
            for dy in (1, 3, 2):
                slab_copy(t, dy, y).start()
            share_copy(t, 0).start()

    def share(t):
        @pl.when(collects)
        def _():
            for dy in (1, 3, 2):
                slab_copy(t, dy, ys[NY - dy]).wait_recv()
                share_copy(t, dy).start()

        @pl.when(jnp.logical_not(collects))
        def _():
            for dy in range(NY):
                share_copy(t, dy).wait_recv()

    place[...] = spread()
    piece[0] = dot(place[...], tok_in[...], 0, 1).astype(BF16)
    piece_start(0)
    piece[1] = dot(place[...], cot_in[...], 0, 1).astype(BF16)
    piece_start(1)
    for j in range(4):
        gap = slice(PITCH * j + SENT, PITCH * (j + 1))
        for u in (KV, Q, OUT):
            w[u, gap, :] = jnp.zeros((PITCH - SENT, 512), BF16)
        for t in (0, 1):
            slabs[t, gap, :] = jnp.zeros((PITCH - SENT, SUPER), BF16)
            last[t, gap, :] = jnp.zeros((PITCH - SENT, TOK), BF16)

    def rs_copy(u, step, side):
        if step == 1:
            rows = pl.ds(TOK * side, TOK)
            src, dst = part.at[u, zs[4], rows], sum_half.at[u, side]
        else:
            to = zs[5 - step] if side == 0 else zs[3 + step]
            src, dst = part.at[u, to], sum_full.at[u, side, step - 2]
        return remote(
            src, dst, s_rs.at[u, side, step - 1], r_rs.at[u, side, step - 1], z_row(side), col
        )

    def rs_step(u, step):
        for side in (0, 1):
            if step > 1:
                rs_copy(u, step - 1, side).wait_recv()
                to = zs[5 - step] if side == 0 else zs[3 + step]
                if step == 2:
                    rows = slice(TOK * side, TOK * side + TOK)
                    part[u, to, rows] = (
                        part[u, to, rows].astype(F32) + sum_half[u, side].astype(F32)
                    ).astype(BF16)
                else:
                    part[u, to] = (
                        part[u, to].astype(F32) + sum_full[u, side, step - 3].astype(F32)
                    ).astype(BF16)
            rs_copy(u, step, side).start()

    def rs_total(u):
        rs_copy(u, 4, 0).wait_recv()
        rs_copy(u, 4, 1).wait_recv()
        return (
            part[u, z].astype(F32)
            + sum_full[u, 0, 2].astype(F32)
            + sum_full[u, 1, 2].astype(F32)
        ).astype(BF16)

    def ag_copy(v, step, side, sending):
        back = step - 1 if sending else step
        slot = zs[(NZ - back) % NZ] if side == 0 else zs[back]
        if step == 4:
            rows = pl.ds(TOK * side, TOK)
            block = gath.at[v, slot, rows]
        else:
            block = gath.at[v, slot]
        return remote(
            block, block, s_ag.at[v, side, step - 1], r_ag.at[v, side, step - 1], z_row(side), col
        )

    def ag_step(v, step):
        for side in (0, 1):
            if step > 1:
                ag_copy(v, step - 1, side, False).wait_recv()
            if step < 5:
                ag_copy(v, step, side, True).start()

    def gathered(v, h):
        return gath[v, 4 * h : 4 * h + 4].reshape(SUPER, SLAB)

    def project(u, t):
        for h in (0, 1):
            part[u, 4 * h : 4 * h + 4] = (
                dot(slabs[t], w[u, :, 256 * h : 256 * h + 256], 0, 0)
                .astype(BF16)
                .reshape(4, SLAB, SLAB)
            )

    weight_forward(KV)
    collect(0)
    weight_forward(Q)
    share(0)
    weight_wait(KV)
    project(KV, 0)
    rs_step(KV, 1)
    weight_wait(Q)
    project(Q, 0)
    rs_step(Q, 1)
    collect(1)
    weight_forward(OUT)
    rs_step(KV, 2)
    rs_step(Q, 2)
    rs_step(KV, 3)
    share(1)
    weight_wait(OUT)
    rs_step(Q, 3)
    rs_step(KV, 4)
    project(OUT, 1)
    rs_step(OUT, 1)
    rs_step(Q, 4)

    own_keys = pl.ds(BACK * SLAB, SLAB)
    kvwin[own_keys, :] = rs_total(KV)

    def kv_copy(i):
        return remote(
            kvwin.at[own_keys], kvwin.at[pl.ds((BACK - i) * SLAB, SLAB)],
            s_kv.at[i - 1], r_kv.at[i - 1], token_row(i), col,
        )

    for i in range(1, BACK + 1):
        kv_copy(i).start()
    rs_step(OUT, 2)

    def scale_of(values):
        return lax.rsqrt(jnp.mean(values * values, axis=-1, keepdims=True) + epsilon)

    qgain = qg_ref[...] * query_scalar ** (-0.5)
    kgain = kg_ref[...]
    q_raw[...] = rs_total(Q)
    for r in range(2):
        q = q_raw[:, HD * r : HD * r + HD].astype(F32)
        qh[SLAB * r : SLAB * r + SLAB, :] = (q * scale_of(q) * qgain).astype(BF16)
    rs_step(OUT, 3)

    for i in range(1, BACK + 1):
        kv_copy(i).wait_recv()


    @pl.loop(0, BACK + 1)
    def _(s):
        rows = pl.ds(pl.multiple_of(s * SLAB, SLAB), SLAB)
        k = kvwin[rows, 0:HD].astype(F32)
        kh[rows, :] = (k * scale_of(k) * kgain).astype(BF16)

    scores[...] = dot(qh[...], kh[...], 1, 1)
    rs_step(OUT, 4)
    chunk = 32
    first_key = WINDOW - SLAB * place_in_ring

    @pl.loop(0, 2 * SLAB // chunk)
    def _(n):
        rows = pl.ds(pl.multiple_of(n * chunk, chunk), chunk)
        t0 = lax.rem(n, SLAB // chunk) * chunk
        t = t0 + lax.broadcasted_iota(jnp.int32, (chunk, 1), 0)
        key = lax.broadcasted_iota(jnp.int32, (chunk, KEYS), 1)
        allowed = (key <= t + WINDOW) & (key >= jnp.maximum(t + 1, first_key))
        s = jnp.where(allowed, scores[rows, :], -1e30)
        e = jnp.exp(s - jnp.max(s, axis=-1, keepdims=True))
        pb[rows, :] = (e * (1.0 / jnp.sum(e, axis=-1, keepdims=True))).astype(BF16)

    blended = dot(pb[...], kvwin[:, HD:], 1, 0).astype(BF16)
    for r in range(2):
        gath[ATT, z, :, HD * r : HD * r + HD] = blended[SLAB * r : SLAB * r + SLAB]
    ag_step(ATT, 1)

    total = rs_total(OUT)
    for r in range(2):
        datt[SLAB * r : SLAB * r + SLAB, :] = total[:, HD * r : HD * r + HD]

    scores[...] = dot(datt[...], kvwin[:, HD:], 1, 1)
    ag_step(ATT, 2)

    @pl.loop(0, 2 * SLAB // chunk)
    def _(n):
        rows = pl.ds(pl.multiple_of(n * chunk, chunk), chunk)
        p = pb[rows, :].astype(F32)
        dp = scores[rows, :]
        delta = jnp.sum(p * dp, axis=-1, keepdims=True)
        ds[rows, :] = (p * (dp - delta)).astype(BF16)

    ag_step(ATT, 3)

    def norm_back(raw, gain, grad):
        r = scale_of(raw)
        inner = grad * gain
        return r * inner - raw * (r * r * r * jnp.mean(raw * inner, axis=-1, keepdims=True))

    dkh = dot(ds[...], qh[...], 0, 0)
    dvh = dot(pb[...], datt[...], 0, 0)
    for s in range(BACK + 1):
        rows = slice(s * SLAB, s * SLAB + SLAB)
        dk = norm_back(kvwin[rows, 0:HD].astype(F32), kgain, dkh[rows])
        if s == BACK:
            dkv_own[:, 0:HD] = dk
            dkv_own[:, HD:] = dvh[rows]
        else:
            dkv[s, :, 0:HD] = dk.astype(BF16)
            dkv[s, :, HD:] = dvh[rows].astype(BF16)

    def dk_copy(i):
        return remote(
            dkv.at[BACK - i], dkv_in.at[i - 1], s_dk.at[i - 1], r_dk.at[i - 1], token_row(-i), col
        )

    for i in range(1, BACK + 1):
        dk_copy(i).start()
    ag_step(ATT, 4)

    dqh = dot(ds[...], kh[...], 1, 0)
    for r in range(2):
        lanes = slice(HD * r, HD * r + HD)
        gath[DQ, z, :, lanes] = norm_back(
            q_raw[:, lanes].astype(F32), qgain, dqh[SLAB * r : SLAB * r + SLAB]
        ).astype(BF16)
    ag_step(DQ, 1)
    ag_step(ATT, 5)

    def rl_copy(u, side):
        return remote(
            g.at[u, rows_at(xs[2]), pl.ds(256 * side, 256)], relay.at[u, side],
            s_rl.at[u, side], r_rl.at[u, side], x_row(side), col,
        )

    def fl_copy(u, side):
        return remote(
            g.at[u, rows_at(xs[1] if side == 0 else xs[3])], full.at[u, side],
            s_fl.at[u, side], r_fl.at[u, side], x_row(side), col,
        )

    def grad_start(u, t, v):
        for h in (0, 1):
            g[u, :, 256 * h : 256 * h + 256] = dot(slabs[t], gathered(v, h), 1, 0).astype(BF16)
        rl_copy(u, 0).start()
        rl_copy(u, 1).start()

    def grad_middle(u):
        for side in (0, 1):
            rl_copy(u, side).wait_recv()
            rows = rows_at(xs[1] if side == 0 else xs[3])
            lanes = slice(256 * side, 256 * side + 256)
            g[u, rows, lanes] = (
                g[u, rows, lanes].astype(F32) + relay[u, side].astype(F32)
            ).astype(BF16)
            fl_copy(u, side).start()

    def grad_last(u):
        fl_copy(u, 0).wait_recv()
        fl_copy(u, 1).wait_recv()
        total = (
            g[u, own_rows, :].astype(F32)
            + full[u, 0].astype(F32)
            + full[u, 1].astype(F32)
        ).astype(BF16)
        return total[0:OWN]

    def os_copy(t, i):
        return remote(
            ypart.at[t, rows_at(i)], ysib.at[t, i], s_os.at[t, i], r_os.at[t, i], row, sibling
        )

    def oy_copy(t, dy):
        return remote(
            ypart.at[t, rows_at(ys[dy])], yrecv.at[t, dy - 1],
            s_oy.at[t, dy], r_oy.at[t, dy], row, 2 * ys[dy] + core,
        )

    def oz_copy(t, zt):
        return remote(
            ypart.at[t, rows_at(y), lanes_at(zt)], last.at[t, rows_at(quarter)],
            s_oz.at[t, zt], r_oz.at[t, quarter], x * NZ + zt, col,
        )

    def oz_recv(t, j):
        slot = last.at[t, pl.ds(PITCH * j, SENT)]
        return remote(slot, slot, s_oz.at[t, 0], r_oz.at[t, j], x * NZ + 4 * core + j, col)

    def out_start(t):
        @pl.when(jnp.logical_not(collects))
        def _():
            for i in range(NX):
                os_copy(t, i).start()

    def out_middle(t):
        @pl.when(collects)
        def _():
            for dy in (2, 1, 3, 0):
                os_copy(t, ys[dy]).wait_recv()
                rows = rows_at(ys[dy])
                ypart[t, rows, :] = (
                    ypart[t, rows, :].astype(F32) + ysib[t, ys[dy]].astype(F32)
                ).astype(BF16)
                if dy:
                    oy_copy(t, dy).start()

    def out_sum(t):
        @pl.when(collects)
        def _():
            for dy in (1, 3, 2):
                oy_copy(t, dy).wait_recv()
            rows = rows_at(y)
            total = ypart[t, rows, :].astype(F32)
            for dy in (1, 2, 3):
                total = total + yrecv[t, dy - 1].astype(F32)
            ypart[t, rows, :] = total.astype(BF16)
            for d in (4, 3, 5, 2, 6, 1, 7):
                oz_copy(t, zs[d]).start()
            last[t, rows_at(quarter), :] = ypart[t, rows, lanes_at(z)]

    def out_last(t, out):
        for j in range(4):
            @pl.when(4 * core + j != z)
            def _():
                oz_recv(t, j).wait_recv()
        out[...] = dot(last[t], place[...], 0, 1).astype(BF16)

    grad_start(OUT, 1, ATT)
    ag_step(DQ, 2)
    ypart[0] = (
        dot(w[OUT, :, 0:256], gathered(ATT, 0), 1, 1)
        + dot(w[OUT, :, 256:512], gathered(ATT, 1), 1, 1)
    ).astype(BF16)
    out_start(0)
    ag_step(DQ, 3)

    for i in range(1, BACK + 1):
        dk_copy(i).wait_recv()
    total = dkv_own[...]
    for i in range(BACK):
        total = total + dkv_in[i].astype(F32)
    gath[DKV, z] = total.astype(BF16)
    ag_step(DKV, 1)

    grad_middle(OUT)
    ag_step(DQ, 4)
    ag_step(DKV, 2)
    out_middle(0)
    ag_step(DQ, 5)
    grad_start(Q, 0, DQ)
    ag_step(DKV, 3)
    ag_step(DKV, 4)
    out_sum(0)
    grad_middle(Q)
    ag_step(DKV, 5)
    grad_start(KV, 0, DKV)
    total = (
        dot(w[Q, :, 0:256], gathered(DQ, 0), 1, 1) + dot(w[Q, :, 256:512], gathered(DQ, 1), 1, 1)
    )
    ypart[1] = (
        total
        + dot(w[KV, :, 0:256], gathered(DKV, 0), 1, 1)
        + dot(w[KV, :, 256:512], gathered(DKV, 1), 1, 1)
    ).astype(BF16)
    out_start(1)
    grad_middle(KV)
    out_middle(1)
    go_out[...] = grad_last(OUT)
    out_last(0, layer_out)
    out_sum(1)
    gq_out[...] = grad_last(Q)
    done = grad_last(KV)
    for h in (0, 1):
        gk_out[:, 128 * h : 128 * h + 128] = done[:, 256 * h : 256 * h + 128]
        gv_out[:, 128 * h : 128 * h + 128] = done[:, 256 * h + 128 : 256 * h + 256]
    out_last(1, input_grad)

    for u in (KV, Q, OUT):
        for side in (0, 1):
            xf_copy(u, side, x).wait_send()
            xh_copy(u, side, xs[3] if side == 0 else xs[1]).wait_send()
            rl_copy(u, side).wait_send()
            fl_copy(u, side).wait_send()
            for step in range(1, 5):
                rs_copy(u, step, side).wait_send()
                ag_copy(u, step, side, True).wait_send()
    for t in (0, 1):
        for j in range(4):
            @pl.when(4 * core + j != z)
            def _():
                piece_copy(t, j, 4 * core + j).wait_send()

        @pl.when(collects)
        def _():
            for dy in (1, 2, 3):
                slab_copy(t, dy, y).wait_send()
                oy_copy(t, dy).wait_send()
            for dy in range(NY):
                share_copy(t, dy).wait_send()
            for d in range(1, NZ):
                oz_copy(t, zs[d]).wait_send()

        @pl.when(jnp.logical_not(collects))
        def _():
            for i in range(NX):
                os_copy(t, i).wait_send()

    for i in range(1, BACK + 1):
        kv_copy(i).wait_send()
        dk_copy(i).wait_send()


def shards(tokens, w_query, w_key, w_value, w_output, query_gain, key_gain, cotangent):
    vmem = lambda *shape, dtype=BF16: pltpu.VMEM(shape, dtype)
    dma = lambda *shape: pltpu.SemaphoreType.DMA(shape)
    spec = pl.BlockSpec(memory_space=pltpu.VMEM)
    scratch = [
        vmem(4 * OWN, BLOCK), vmem(2, BLOCK, TOK), vmem(2, BLOCK, SUPER),
        vmem(3, BLOCK, 512), vmem(3, BLOCK, 512),
        vmem(3, NZ, SLAB, SLAB), vmem(3, 2, TOK, SLAB), vmem(3, 2, 3, SLAB, SLAB),
        vmem(3, NZ, SLAB, SLAB),
        vmem(SLAB, SLAB), vmem(2 * SLAB, HD), vmem(KEYS, HD), vmem(KEYS, 2 * HD),
        vmem(2 * SLAB, KEYS, dtype=F32), vmem(2 * SLAB, KEYS), vmem(2 * SLAB, KEYS),
        vmem(2 * SLAB, HD),
        vmem(BACK, SLAB, 256), vmem(SLAB, 256, dtype=F32), vmem(BACK, SLAB, 256),
        vmem(2, BLOCK, SUPER), vmem(2, NX, SENT, SUPER), vmem(2, 3, SENT, SUPER),
        vmem(2, BLOCK, TOK), vmem(3, 2, SENT, 256), vmem(3, 2, SENT, 512),
        dma(3, 2), dma(3, 2), dma(3, 2), dma(3, 2),
        dma(2, 4), dma(2, NZ), dma(2, NY), dma(2, NY), dma(2, NY), dma(2, NY), dma(2),
        dma(3, 2, 4), dma(3, 2, 4), dma(3, 2, 4), dma(3, 2, 4), dma(1), dma(1),
        dma(BACK), dma(BACK), dma(BACK), dma(BACK),
        dma(3, 2), dma(3, 2), dma(3, 2), dma(3, 2),
        dma(2, NX), dma(2, NX), dma(2, NY), dma(2, NY), dma(2, NZ), dma(2, 4),
    ]
    outs = [
        jax.ShapeDtypeStruct(tokens.shape, BF16),
        jax.ShapeDtypeStruct(tokens.shape, BF16),
        jax.ShapeDtypeStruct(w_query.shape, BF16),
        jax.ShapeDtypeStruct(w_key.shape, BF16),
        jax.ShapeDtypeStruct(w_value.shape, BF16),
        jax.ShapeDtypeStruct(w_output.shape[::-1], BF16),
    ]
    layer_out, input_grad, gq, gk, gv, go = pl.pallas_call(
        kernel,
        out_shape=outs,
        in_specs=[spec] * 8,
        out_specs=[spec] * 6,
        scratch_shapes=scratch,
        compiler_params=pltpu.CompilerParams(
            collective_id=0, has_side_effects=True, vmem_limit_bytes=60 * 1024 * 1024
        ),
    )(
        tokens, cotangent, w_query, w_key, w_value, w_output.T,
        query_gain.reshape(1, HD), key_gain.reshape(1, HD),
    )
    return layer_out, input_grad, gq, gk, gv, go.T


def solution(mesh):
    in_specs = (
        P("row", "col"), P("row", "col"), P("row", "col"), P("row", "col"), P("col", "row"),
        P(), P(), P("row", "col"),
    )
    out_specs = (
        P("row", "col"), P("row", "col"), P("row", "col"), P("row", "col"), P("row", "col"),
        P("col", "row"),
    )
    return jax.shard_map(shards, mesh=mesh, in_specs=in_specs, out_specs=out_specs, check_vma=False)
```

```python
import jax
import jax.numpy as jnp
from jax import lax
from jax.experimental import pallas as pl
from jax.experimental.pallas import tpu as pltpu
from jax.sharding import PartitionSpec as P

BF16 = jnp.bfloat16
F32 = jnp.float32

NX, NZ, NY = 4, 8, 4

OWN, SENT, PITCH, BLOCK = 168, 176, 192, 768
TOK = 128
SUPER = 1024
SLAB = 256
HD = 128
BACK = 4
KEYS = (BACK + 1) * SLAB
WINDOW = 1024
KV, Q, OUT = 0, 1, 2
ATT, DQ, DKV = 0, 1, 2
query_scalar = 168.0
epsilon = 1e-06


def dot(a, b, ca, cb):
    return lax.dot_general(a, b, (((ca,), (cb,)), ((), ())), preferred_element_type=F32)


def ring(a, n):
    return lax.rem(a + n, n)


def kernel(
    tok_in, cot_in, wq_in, wk_in, wv_in, wo_in, qg_ref, kg_ref,
    layer_out, input_grad, gq_out, gk_out, gv_out, go_out,
    piece, slabs, w, g, part, sum_half, sum_full, gath,
    q_raw, qh, kh, kvwin, scores, pb, ds, datt, dkv, dkv_own, dkv_in,
    ypart, rest, ysib, yrecv, last, relay, full,
    s_xf, r_xf, s_xh, r_xh, s_p, r_p, s_y, r_y, s_s, r_s,
    s_rs, r_rs, s_ag, r_ag, s_kv, r_kv, s_dk, r_dk,
    s_rl, r_rl, s_fl, r_fl, s_os, r_os, s_oy, r_oy, s_oz, r_oz,
):
    row = lax.axis_index("row")
    col = lax.axis_index("col")
    x, z = lax.div(row, NZ), lax.rem(row, NZ)
    y, core = lax.div(col, 2), lax.rem(col, 2)
    head, quarter = lax.div(z, 4), lax.rem(z, 4)
    xs = [ring(x + d, NX) for d in range(NX)]
    zs = [ring(z + d, NZ) for d in range(NZ)]
    ys = [ring(y + d, NY) for d in range(NY)]
    sibling = col + 1 - 2 * core
    place_in_ring = 4 * x + quarter

    def remote(src, dst, ssem, rsem, to_row, to_col):
        return pltpu.make_async_remote_copy(
            src_ref=src, dst_ref=dst, send_sem=ssem, recv_sem=rsem,
            device_id={"row": to_row, "col": to_col}, device_id_type=pl.DeviceIdType.MESH,
        )

    def token_row(i):
        at = lax.rem(place_in_ring + 16 + i, 16)
        return lax.div(at, 4) * NZ + 4 * head + lax.rem(at, 4)

    def x_row(side):
        return (xs[1] if side == 0 else xs[3]) * NZ + z

    def z_row(side):
        return x * NZ + (zs[1] if side == 0 else zs[7])

    barrier = pltpu.get_barrier_semaphore()

    def greet(to_row, to_col):
        pl.semaphore_signal(
            barrier, inc=1, device_id={"row": to_row, "col": to_col},
            device_id_type=pl.DeviceIdType.MESH,
        )

    at_home = core == head
    for j in range(4):
        @pl.when(4 * core + j != z)
        def _():
            greet(x * NZ + 4 * core + j, 2 * y + head)

    greet(z_row(0), col)
    greet(z_row(1), col)
    for d in range(1, NY):
        greet(row, 2 * ys[d] + core)
    for i in range(1, BACK + 1):
        greet(token_row(i), col)
        greet(token_row(-i), col)
    greet(row, sibling)
    greet(x_row(0), col)
    greet(x_row(1), col)

    def rows_at(i):
        return pl.ds(pl.multiple_of(PITCH * i, 16), SENT)

    own_rows = rows_at(x)
    for u in (KV, Q, OUT):
        w[u, pl.ds(pl.multiple_of(PITCH * x + 160, 16), 16), :] = jnp.zeros((16, 512), BF16)
    weight_rows = pl.ds(pl.multiple_of(PITCH * x, 16), OWN)
    for h in (0, 1):
        w[KV, weight_rows, 256 * h : 256 * h + 128] = wk_in[:, 128 * h : 128 * h + 128]
        w[KV, weight_rows, 256 * h + 128 : 256 * h + 256] = wv_in[:, 128 * h : 128 * h + 128]
    w[Q, weight_rows, :] = wq_in[...]
    w[OUT, weight_rows, :] = wo_in[...]

    pl.semaphore_wait(barrier, 20 - at_home.astype(jnp.int32))

    def xf_copy(u, side, xx):
        slot = w.at[u, rows_at(xx)]
        return remote(slot, slot, s_xf.at[u, side], r_xf.at[u, side], x_row(side), col)

    def xh_copy(u, side, xx):
        slot = w.at[u, rows_at(xx), pl.ds(256 * side, 256)]
        return remote(slot, slot, s_xh.at[u, side], r_xh.at[u, side], x_row(side), col)

    def weight_start(u):
        xf_copy(u, 0, x).start()
        xf_copy(u, 1, x).start()

    def weight_forward(u):
        xf_copy(u, 0, xs[3]).wait_recv()
        xh_copy(u, 0, xs[3]).start()
        xf_copy(u, 1, xs[1]).wait_recv()
        xh_copy(u, 1, xs[1]).start()

    def weight_wait(u):
        xh_copy(u, 0, xs[2]).wait_recv()
        xh_copy(u, 1, xs[2]).wait_recv()

    weight_start(KV)

    def lanes_at(i):
        return pl.ds(pl.multiple_of(TOK * i, TOK), TOK)

    def half_at(c):
        return pl.ds(pl.multiple_of(512 * c, 512), 512)

    def piece_copy(t, j):
        return remote(
            piece.at[t, pl.ds(PITCH * j, SENT)], slabs.at[t, rows_at(y), lanes_at(z)],
            s_p.at[t, j], r_p.at[t, quarter], x * NZ + 4 * core + j, 2 * y + head,
        )

    def piece_recv(t, j):
        slot = slabs.at[t, rows_at(y), lanes_at(4 * core + j)]
        return remote(
            slot, slot, s_p.at[t, j], r_p.at[t, j], x * NZ + 4 * core + j, 2 * y + head
        )

    def piece_start(t):
        for j in range(4):
            @pl.when(4 * core + j != z)
            def _():
                piece_copy(t, j).start()

            @pl.when(4 * core + j == z)
            def _():
                slabs[t, rows_at(y), lanes_at(z)] = piece[t, PITCH * j : PITCH * j + SENT]

    def slab_copy(t, dy, yy):
        slot = slabs.at[t, rows_at(yy), half_at(core)]
        return remote(slot, slot, s_y.at[t, dy], r_y.at[t, dy], row, 2 * ys[dy] + core)

    def share_copy(t, dy, cc):
        slot = slabs.at[t, rows_at(ys[(NY - dy) % NY]), half_at(cc)]
        return remote(slot, slot, s_s.at[t, dy], r_s.at[t, dy], row, sibling)

    def collect(t):
        for j in range(4):
            @pl.when(4 * core + j != z)
            def _():
                piece_recv(t, j).wait_recv()
        for dy in (2, 1, 3):
            slab_copy(t, dy, y).start()
        share_copy(t, 0, core).start()

    def share(t):
        for dy in (1, 3, 2):
            slab_copy(t, dy, ys[NY - dy]).wait_recv()
            share_copy(t, dy, core).start()
        for dy in (0, 1, 3, 2):
            share_copy(t, dy, 1 - core).wait_recv()

    for t, src in ((0, tok_in), (1, cot_in)):
        for j in range(4):
            piece[t, PITCH * j + 160 : PITCH * j + SENT] = jnp.zeros((SENT - 160, TOK), BF16)
            piece[t, PITCH * j : PITCH * j + OWN] = src[OWN * j : OWN * j + OWN]
        piece_start(t)
        if t == 0:
            weight_start(Q)
    for j in range(4):
        gap = slice(PITCH * j + SENT, PITCH * (j + 1))
        for u in (KV, Q, OUT):
            w[u, gap, :] = jnp.zeros((PITCH - SENT, 512), BF16)
        for t in (0, 1):
            slabs[t, gap, :] = jnp.zeros((PITCH - SENT, SUPER), BF16)

    def rs_copy(u, step, side):
        if step == 1:
            rows = pl.ds(TOK * side, TOK)
            src, dst = part.at[u, zs[4], rows], sum_half.at[u, side]
        else:
            to = zs[5 - step] if side == 0 else zs[3 + step]
            src, dst = part.at[u, to], sum_full.at[u, side, step - 2]
        return remote(
            src, dst, s_rs.at[u, side, step - 1], r_rs.at[u, side, step - 1], z_row(side), col
        )

    def rs_step(u, step):
        for side in (0, 1):
            if step > 1:
                rs_copy(u, step - 1, side).wait_recv()
                to = zs[5 - step] if side == 0 else zs[3 + step]
                if step == 2:
                    rows = slice(TOK * side, TOK * side + TOK)
                    part[u, to, rows] = (
                        part[u, to, rows].astype(F32) + sum_half[u, side].astype(F32)
                    ).astype(BF16)
                else:
                    part[u, to] = (
                        part[u, to].astype(F32) + sum_full[u, side, step - 3].astype(F32)
                    ).astype(BF16)
            rs_copy(u, step, side).start()

    def rs_total(u):
        rs_copy(u, 4, 0).wait_recv()
        rs_copy(u, 4, 1).wait_recv()
        return (
            part[u, z].astype(F32)
            + sum_full[u, 0, 2].astype(F32)
            + sum_full[u, 1, 2].astype(F32)
        ).astype(BF16)

    def ag_copy(v, step, side, sending):
        back = step - 1 if sending else step
        slot = zs[(NZ - back) % NZ] if side == 0 else zs[back]
        if step == 4:
            rows = pl.ds(TOK * side, TOK)
            block = gath.at[v, slot, rows]
        else:
            block = gath.at[v, slot]
        return remote(
            block, block, s_ag.at[v, side, step - 1], r_ag.at[v, side, step - 1], z_row(side), col
        )

    def ag_step(v, step):
        for side in (0, 1):
            if step > 1:
                ag_copy(v, step - 1, side, False).wait_recv()
            if step < 5:
                ag_copy(v, step, side, True).start()

    def gathered(v, h):
        return gath[v, 4 * h : 4 * h + 4].reshape(SUPER, SLAB)

    def project(u, t):
        for h in (0, 1):
            part[u, 4 * h : 4 * h + 4] = (
                dot(slabs[t], w[u, :, 256 * h : 256 * h + 256], 0, 0)
                .astype(BF16)
                .reshape(4, SLAB, SLAB)
            )

    collect(0)
    weight_forward(KV)
    weight_forward(Q)
    collect(1)
    weight_start(OUT)
    share(0)
    weight_wait(KV)
    project(KV, 0)
    rs_step(KV, 1)
    weight_wait(Q)
    project(Q, 0)
    rs_step(KV, 2)
    rs_step(Q, 1)
    weight_forward(OUT)
    share(1)
    rs_step(KV, 3)
    rs_step(Q, 2)
    weight_wait(OUT)
    project(OUT, 1)
    rs_step(KV, 4)
    rs_step(Q, 3)
    rs_step(OUT, 1)
    own_keys = pl.ds(BACK * SLAB, SLAB)
    kvwin[own_keys, :] = rs_total(KV)

    def kv_copy(i):
        return remote(
            kvwin.at[own_keys], kvwin.at[pl.ds((BACK - i) * SLAB, SLAB)],
            s_kv.at[i - 1], r_kv.at[i - 1], token_row(i), col,
        )

    for i in range(1, BACK + 1):
        kv_copy(i).start()
    rs_step(Q, 4)
    rs_step(OUT, 2)

    def scale_of(values):
        return lax.rsqrt(jnp.mean(values * values, axis=-1, keepdims=True) + epsilon)

    qgain = qg_ref[...] * query_scalar ** (-0.5)
    kgain = kg_ref[...]
    q_raw[...] = rs_total(Q)
    for r in range(2):
        q = q_raw[:, HD * r : HD * r + HD].astype(F32)
        qh[SLAB * r : SLAB * r + SLAB, :] = (q * scale_of(q) * qgain).astype(BF16)

    for i in range(1, BACK + 1):
        kv_copy(i).wait_recv()


    @pl.loop(0, BACK + 1)
    def _(s):
        rows = pl.ds(pl.multiple_of(s * SLAB, SLAB), SLAB)
        k = kvwin[rows, 0:HD].astype(F32)
        kh[rows, :] = (k * scale_of(k) * kgain).astype(BF16)

    scores[...] = dot(qh[...], kh[...], 1, 1)
    rs_step(OUT, 3)
    chunk = 32
    first_key = WINDOW - SLAB * place_in_ring

    def softmax(n):
        rows = pl.ds(pl.multiple_of(n * chunk, chunk), chunk)
        t0 = lax.rem(n, SLAB // chunk) * chunk
        t = t0 + lax.broadcasted_iota(jnp.int32, (chunk, 1), 0)
        key = lax.broadcasted_iota(jnp.int32, (chunk, KEYS), 1)
        allowed = (key <= t + WINDOW) & (key >= jnp.maximum(t + 1, first_key))
        s = jnp.where(allowed, scores[rows, :], -1e30)
        e = jnp.exp(s - jnp.max(s, axis=-1, keepdims=True))
        pb[rows, :] = (e * (1.0 / jnp.sum(e, axis=-1, keepdims=True))).astype(BF16)

    pl.loop(0, SLAB // chunk)(softmax)
    rs_step(OUT, 4)
    pl.loop(SLAB // chunk, 2 * SLAB // chunk)(softmax)
    blended = dot(pb[...], kvwin[:, HD:], 1, 0).astype(BF16)
    for r in range(2):
        gath[ATT, z, :, HD * r : HD * r + HD] = blended[SLAB * r : SLAB * r + SLAB]
    ag_step(ATT, 1)

    total = rs_total(OUT)
    for r in range(2):
        datt[SLAB * r : SLAB * r + SLAB, :] = total[:, HD * r : HD * r + HD]

    scores[...] = dot(datt[...], kvwin[:, HD:], 1, 1)

    def softmax_back(n):
        rows = pl.ds(pl.multiple_of(n * chunk, chunk), chunk)
        p = pb[rows, :].astype(F32)
        dp = scores[rows, :]
        delta = jnp.sum(p * dp, axis=-1, keepdims=True)
        ds[rows, :] = (p * (dp - delta)).astype(BF16)

    pl.loop(0, 2 * SLAB // chunk)(softmax_back)

    def norm_back(raw, gain, grad):
        r = scale_of(raw)
        inner = grad * gain
        return r * inner - raw * (r * r * r * jnp.mean(raw * inner, axis=-1, keepdims=True))

    dkh = dot(ds[...], qh[...], 0, 0)
    dvh = dot(pb[...], datt[...], 0, 0)
    for s in range(BACK + 1):
        rows = slice(s * SLAB, s * SLAB + SLAB)
        dk = norm_back(kvwin[rows, 0:HD].astype(F32), kgain, dkh[rows])
        if s == BACK:
            dkv_own[:, 0:HD] = dk
            dkv_own[:, HD:] = dvh[rows]
        else:
            dkv[s, :, 0:HD] = dk.astype(BF16)
            dkv[s, :, HD:] = dvh[rows].astype(BF16)

    def dk_copy(i):
        return remote(
            dkv.at[BACK - i], dkv_in.at[i - 1], s_dk.at[i - 1], r_dk.at[i - 1], token_row(-i), col
        )

    for i in range(1, BACK + 1):
        dk_copy(i).start()
    ag_step(ATT, 2)

    dqh = dot(ds[...], kh[...], 1, 0)
    for r in range(2):
        lanes = slice(HD * r, HD * r + HD)
        gath[DQ, z, :, lanes] = norm_back(
            q_raw[:, lanes].astype(F32), qgain, dqh[SLAB * r : SLAB * r + SLAB]
        ).astype(BF16)
    ag_step(DQ, 1)
    ag_step(ATT, 3)
    ag_step(DQ, 2)
    ag_step(ATT, 4)

    def rl_copy(u, side):
        return remote(
            g.at[u, rows_at(xs[2]), pl.ds(256 * side, 256)], relay.at[u, side],
            s_rl.at[u, side], r_rl.at[u, side], x_row(side), col,
        )

    def fl_copy(u, side):
        return remote(
            g.at[u, rows_at(xs[1] if side == 0 else xs[3])], full.at[u, side],
            s_fl.at[u, side], r_fl.at[u, side], x_row(side), col,
        )

    def grad_start(u, t, v):
        for h in (0, 1):
            g[u, :, 256 * h : 256 * h + 256] = dot(slabs[t], gathered(v, h), 1, 0).astype(BF16)
        rl_copy(u, 0).start()
        rl_copy(u, 1).start()

    def grad_middle(u):
        for side in (0, 1):
            rl_copy(u, side).wait_recv()
            rows = rows_at(xs[1] if side == 0 else xs[3])
            lanes = slice(256 * side, 256 * side + 256)
            g[u, rows, lanes] = (
                g[u, rows, lanes].astype(F32) + relay[u, side].astype(F32)
            ).astype(BF16)
            fl_copy(u, side).start()

    def grad_last(u):
        fl_copy(u, 0).wait_recv()
        fl_copy(u, 1).wait_recv()
        total = (
            g[u, own_rows, :].astype(F32)
            + full[u, 0].astype(F32)
            + full[u, 1].astype(F32)
        ).astype(BF16)
        return total[0:OWN]

    def os_copy(t, dy, cc):
        return remote(
            ypart.at[t, rows_at(ys[dy]), half_at(1 - cc)], ysib.at[t, dy],
            s_os.at[t, dy], r_os.at[t, dy], row, sibling,
        )

    def oy_copy(t, dy):
        return remote(
            ypart.at[t, rows_at(ys[dy]), half_at(core)], yrecv.at[t, dy - 1],
            s_oy.at[t, dy], r_oy.at[t, dy], row, 2 * ys[dy] + core,
        )

    def oz_copy(t, j):
        return remote(
            ypart.at[t, rows_at(y), lanes_at(4 * core + j)], last.at[t, rows_at(quarter)],
            s_oz.at[t, j], r_oz.at[t, quarter], x * NZ + 4 * core + j, 2 * y + head,
        )

    def oz_recv(t, j):
        slot = last.at[t, pl.ds(PITCH * j, SENT)]
        return remote(
            slot, slot, s_oz.at[t, j], r_oz.at[t, j], x * NZ + 4 * core + j, 2 * y + head
        )

    def out_start(t):
        for dy in (2, 1, 3, 0):
            os_copy(t, dy, core).start()

    def out_middle(t):
        for dy in (2, 1, 3, 0):
            os_copy(t, dy, core).wait_recv()
            rows, lanes = rows_at(ys[dy]), half_at(core)
            ypart[t, rows, lanes] = (
                ypart[t, rows, lanes].astype(F32) + ysib[t, dy].astype(F32)
            ).astype(BF16)
            if dy:
                oy_copy(t, dy).start()

    def out_sum(t):
        for dy in (1, 3, 2):
            oy_copy(t, dy).wait_recv()
        rows, lanes = rows_at(y), half_at(core)
        total = ypart[t, rows, lanes].astype(F32)
        for dy in (1, 2, 3):
            total = total + yrecv[t, dy - 1].astype(F32)
        ypart[t, rows, lanes] = total.astype(BF16)
        for j in range(4):
            @pl.when(4 * core + j != z)
            def _():
                oz_copy(t, j).start()

            @pl.when(4 * core + j == z)
            def _():
                last[t, PITCH * j : PITCH * j + SENT] = ypart[t, rows, lanes_at(z)]

    def out_last(t, out):
        for j in range(4):
            @pl.when(4 * core + j != z)
            def _():
                oz_recv(t, j).wait_recv()
        for j in range(4):
            out[OWN * j : OWN * j + OWN] = last[t, PITCH * j : PITCH * j + OWN]

    for i in range(1, BACK + 1):
        dk_copy(i).wait_recv()
    total = dkv_own[...]
    for i in range(BACK):
        total = total + dkv_in[i].astype(F32)
    gath[DKV, z] = total.astype(BF16)
    ag_step(DKV, 1)
    ag_step(DQ, 3)
    ag_step(ATT, 5)
    grad_start(OUT, 1, ATT)
    ag_step(DKV, 2)
    ag_step(DQ, 4)
    ypart[0] = (
        dot(w[OUT, :, 0:256], gathered(ATT, 0), 1, 1)
        + dot(w[OUT, :, 256:512], gathered(ATT, 1), 1, 1)
    ).astype(BF16)
    out_start(0)
    ag_step(DKV, 3)
    grad_middle(OUT)
    ag_step(DQ, 5)
    out_middle(0)
    ag_step(DKV, 4)
    grad_start(Q, 0, DQ)
    rest[...] = (
        dot(w[Q, :, 0:256], gathered(DQ, 0), 1, 1) + dot(w[Q, :, 256:512], gathered(DQ, 1), 1, 1)
    )
    ag_step(DKV, 5)
    ypart[1] = (
        rest[...]
        + dot(w[KV, :, 0:256], gathered(DKV, 0), 1, 1)
        + dot(w[KV, :, 256:512], gathered(DKV, 1), 1, 1)
    ).astype(BF16)
    out_start(1)
    grad_start(KV, 0, DKV)
    out_middle(1)
    grad_middle(Q)
    grad_middle(KV)
    out_sum(0)
    go_out[...] = grad_last(OUT)
    gq_out[...] = grad_last(Q)
    out_sum(1)
    out_last(0, layer_out)
    done = grad_last(KV)
    for h in (0, 1):
        gk_out[:, 128 * h : 128 * h + 128] = done[:, 256 * h : 256 * h + 128]
        gv_out[:, 128 * h : 128 * h + 128] = done[:, 256 * h + 128 : 256 * h + 256]
    out_last(1, input_grad)

    for u in (KV, Q, OUT):
        for side in (0, 1):
            xf_copy(u, side, x).wait_send()
            xh_copy(u, side, xs[3] if side == 0 else xs[1]).wait_send()
            rl_copy(u, side).wait_send()
            fl_copy(u, side).wait_send()
            for step in range(1, 5):
                rs_copy(u, step, side).wait_send()
                ag_copy(u, step, side, True).wait_send()
    for t in (0, 1):
        for j in range(4):
            @pl.when(4 * core + j != z)
            def _():
                piece_copy(t, j).wait_send()
                oz_copy(t, j).wait_send()
        for dy in range(NY):
            share_copy(t, dy, core).wait_send()
            os_copy(t, dy, core).wait_send()
            if dy:
                slab_copy(t, dy, y).wait_send()
                oy_copy(t, dy).wait_send()

    for i in range(1, BACK + 1):
        kv_copy(i).wait_send()
        dk_copy(i).wait_send()


def hand_over(*refs):
    for source, target in zip(refs[:6], refs[6:]):
        target[...] = source[...]


def shards(tokens, w_query, w_key, w_value, w_output, query_gain, key_gain, cotangent):
    vmem = lambda *shape, dtype=BF16: pltpu.VMEM(shape, dtype)
    dma = lambda *shape: pltpu.SemaphoreType.DMA(shape)
    spec = pl.BlockSpec(memory_space=pltpu.VMEM)
    scratch = [
        vmem(2, BLOCK, TOK), vmem(2, BLOCK, SUPER),
        vmem(3, BLOCK, 512), vmem(3, BLOCK, 512),
        vmem(3, NZ, SLAB, SLAB), vmem(3, 2, TOK, SLAB), vmem(3, 2, 3, SLAB, SLAB),
        vmem(3, NZ, SLAB, SLAB),
        vmem(SLAB, SLAB), vmem(2 * SLAB, HD), vmem(KEYS, HD), vmem(KEYS, 2 * HD),
        vmem(2 * SLAB, KEYS, dtype=F32), vmem(2 * SLAB, KEYS), vmem(2 * SLAB, KEYS),
        vmem(2 * SLAB, HD),
        vmem(BACK, SLAB, 256), vmem(SLAB, 256, dtype=F32), vmem(BACK, SLAB, 256),
        vmem(2, BLOCK, SUPER), vmem(BLOCK, SUPER, dtype=F32),
        vmem(2, NY, SENT, 512), vmem(2, 3, SENT, 512),
        vmem(2, BLOCK, TOK), vmem(3, 2, SENT, 256), vmem(3, 2, SENT, 512),
        dma(3, 2), dma(3, 2), dma(3, 2), dma(3, 2),
        dma(2, 4), dma(2, 4), dma(2, NY), dma(2, NY), dma(2, NY), dma(2, NY),
        dma(3, 2, 4), dma(3, 2, 4), dma(3, 2, 4), dma(3, 2, 4),
        dma(BACK), dma(BACK), dma(BACK), dma(BACK),
        dma(3, 2), dma(3, 2), dma(3, 2), dma(3, 2),
        dma(2, NY), dma(2, NY), dma(2, NY), dma(2, NY), dma(2, 4), dma(2, 4),
    ]
    outs = [
        jax.ShapeDtypeStruct(tokens.shape[::-1], BF16),
        jax.ShapeDtypeStruct(tokens.shape[::-1], BF16),
        jax.ShapeDtypeStruct(w_query.shape, BF16),
        jax.ShapeDtypeStruct(w_key.shape, BF16),
        jax.ShapeDtypeStruct(w_value.shape, BF16),
        jax.ShapeDtypeStruct(w_output.shape[::-1], BF16),
    ]
    results = pl.pallas_call(
        kernel,
        out_shape=outs,
        in_specs=[spec] * 8,
        out_specs=[spec] * 6,
        scratch_shapes=scratch,
        compiler_params=pltpu.CompilerParams(
            collective_id=0, has_side_effects=True, vmem_limit_bytes=60 * 1024 * 1024
        ),
    )(
        tokens.T, cotangent.T, w_query, w_key, w_value, w_output.T,
        query_gain.reshape(1, HD), key_gain.reshape(1, HD),
    )
    layer_out, input_grad, gq, gk, gv, go = pl.pallas_call(
        hand_over, out_shape=outs, in_specs=[spec] * 6, out_specs=[spec] * 6
    )(*results)
    return layer_out.T, input_grad.T, gq, gk, gv, go.T


def solution(mesh):
    in_specs = (
        P("row", "col"), P("row", "col"), P("row", "col"), P("row", "col"), P("col", "row"),
        P(), P(), P("row", "col"),
    )
    out_specs = (
        P("row", "col"), P("row", "col"), P("row", "col"), P("row", "col"), P("row", "col"),
        P("col", "row"),
    )
    return jax.shard_map(shards, mesh=mesh, in_specs=in_specs, out_specs=out_specs, check_vma=False)
```

```python
import jax
import jax.numpy as jnp
from jax import lax
from jax.experimental import pallas as pl
from jax.experimental.pallas import tpu as pltpu
from jax.sharding import PartitionSpec as P

BF16 = jnp.bfloat16
F32 = jnp.float32

NX, NZ, NY = 4, 8, 4

OWN, SENT, PITCH, BLOCK = 168, 176, 192, 768
TOK = 128
SUPER = 1024
SLAB = 256
HD = 128
BACK = 4
KEYS = (BACK + 1) * SLAB
WINDOW = 1024
KV, Q, OUT = 0, 1, 2
ATT, DQ, DKV = 0, 1, 2
query_scalar = 168.0
epsilon = 1e-06


def dot(a, b, ca, cb):
    return lax.dot_general(a, b, (((ca,), (cb,)), ((), ())), preferred_element_type=F32)


def ring(a, n):
    return lax.rem(a + n, n)


def kernel(
    tok_in, cot_in, wq_in, wk_in, wv_in, wo_in, qg_ref, kg_ref,
    layer_out, input_grad, gq_out, gk_out, gv_out, go_out,
    piece, slabs, w, g, part, sums, gath,
    q_raw, qh, kh, kvwin, scores, pb, ds, datt, dkv, dkv_own, dkv_in,
    ypart, rest, ysib, yrecv, last, relay, full,
    s_xf, r_xf, s_xh, r_xh, s_p, r_p, s_y, r_y, s_s, r_s,
    s_rs, r_rs, s_ag, r_ag, s_kv, r_kv, s_dk, r_dk,
    s_rl, r_rl, s_fl, r_fl, s_os, r_os, s_oy, r_oy, s_oz, r_oz,
):
    row = lax.axis_index("row")
    col = lax.axis_index("col")
    x, z = lax.div(row, NZ), lax.rem(row, NZ)
    y, core = lax.div(col, 2), lax.rem(col, 2)
    head, quarter = lax.div(z, 4), lax.rem(z, 4)
    xs = [ring(x + d, NX) for d in range(NX)]
    zs = [ring(z + d, NZ) for d in range(NZ)]
    ys = [ring(y + d, NY) for d in range(NY)]
    sibling = col + 1 - 2 * core
    shift = 2 * core
    ls = [ring(z + shift + d, NZ) for d in range(NZ)]
    lz = ls[0]
    place_in_ring = 4 * x + lax.rem(lz, 4)

    def remote(src, dst, ssem, rsem, to_row, to_col):
        return pltpu.make_async_remote_copy(
            src_ref=src, dst_ref=dst, send_sem=ssem, recv_sem=rsem,
            device_id={"row": to_row, "col": to_col}, device_id_type=pl.DeviceIdType.MESH,
        )

    def token_row(i):
        at = lax.rem(place_in_ring + 16 + i, 16)
        return lax.div(at, 4) * NZ + ring(4 * lax.div(lz, 4) + lax.rem(at, 4) + NZ - shift, NZ)

    def x_row(side):
        return (xs[1] if side == 0 else xs[3]) * NZ + z

    def z_row(side):
        return x * NZ + (zs[1] if side == 0 else zs[7])

    barrier = pltpu.get_barrier_semaphore()

    def greet(to_row, to_col):
        pl.semaphore_signal(
            barrier, inc=1, device_id={"row": to_row, "col": to_col},
            device_id_type=pl.DeviceIdType.MESH,
        )

    at_home = core == head
    for j in range(4):
        @pl.when(4 * core + j != z)
        def _():
            greet(x * NZ + 4 * core + j, 2 * y + head)

    greet(z_row(0), col)
    greet(z_row(1), col)
    for d in range(1, NY):
        greet(row, 2 * ys[d] + core)
    for i in range(1, BACK + 1):
        greet(token_row(i), col)
        greet(token_row(-i), col)
    greet(row, sibling)
    greet(x_row(0), col)
    greet(x_row(1), col)

    def rows_at(i):
        return pl.ds(pl.multiple_of(PITCH * i, 16), SENT)

    own_rows = rows_at(x)
    for u in (KV, Q, OUT):
        w[u, pl.ds(pl.multiple_of(PITCH * x + 160, 16), 16), :] = jnp.zeros((16, 512), BF16)
    weight_rows = pl.ds(pl.multiple_of(PITCH * x, 16), OWN)
    for h in (0, 1):
        w[KV, weight_rows, 256 * h : 256 * h + 128] = wk_in[:, 128 * h : 128 * h + 128]
        w[KV, weight_rows, 256 * h + 128 : 256 * h + 256] = wv_in[:, 128 * h : 128 * h + 128]
    w[Q, weight_rows, :] = wq_in[...]
    w[OUT, weight_rows, :] = wo_in[...]

    for t, src in ((0, tok_in), (1, cot_in)):
        for j in range(4):
            piece[t, PITCH * j + 160 : PITCH * j + SENT] = jnp.zeros((SENT - 160, TOK), BF16)
            piece[t, PITCH * j : PITCH * j + OWN] = src[OWN * j : OWN * j + OWN]

    pl.semaphore_wait(barrier, 20 - at_home.astype(jnp.int32))

    def xf_copy(u, side, xx):
        slot = w.at[u, rows_at(xx)]
        return remote(slot, slot, s_xf.at[u, side], r_xf.at[u, side], x_row(side), col)

    def xh_copy(u, side, xx):
        slot = w.at[u, rows_at(xx), pl.ds(256 * side, 256)]
        return remote(slot, slot, s_xh.at[u, side], r_xh.at[u, side], x_row(side), col)

    def weight_start(u):
        xf_copy(u, 0, x).start()
        xf_copy(u, 1, x).start()

    def weight_forward(u):
        xf_copy(u, 0, xs[3]).wait_recv()
        xh_copy(u, 0, xs[3]).start()
        xf_copy(u, 1, xs[1]).wait_recv()
        xh_copy(u, 1, xs[1]).start()

    def weight_wait(u):
        xh_copy(u, 0, xs[2]).wait_recv()
        xh_copy(u, 1, xs[2]).wait_recv()

    weight_start(KV)

    def lanes_at(i):
        return pl.ds(pl.multiple_of(TOK * i, TOK), TOK)

    def half_at(c):
        return pl.ds(pl.multiple_of(512 * c, 512), 512)

    def piece_copy(t, j):
        return remote(
            piece.at[t, pl.ds(PITCH * j, SENT)], slabs.at[t, rows_at(y), lanes_at(z)],
            s_p.at[t, j], r_p.at[t, quarter], x * NZ + 4 * core + j, 2 * y + head,
        )

    def piece_recv(t, j):
        slot = slabs.at[t, rows_at(y), lanes_at(4 * core + j)]
        return remote(
            slot, slot, s_p.at[t, 0], r_p.at[t, j], x * NZ + 4 * core + j, 2 * y + head
        )

    def piece_start(t):
        for j in range(4):
            @pl.when(4 * core + j != z)
            def _():
                piece_copy(t, j).start()

            @pl.when(4 * core + j == z)
            def _():
                slabs[t, rows_at(y), lanes_at(z)] = piece[t, PITCH * j : PITCH * j + SENT]

    def slab_copy(t, dy, j, yy):
        slot = slabs.at[t, rows_at(yy), lanes_at(4 * core + j)]
        return remote(slot, slot, s_y.at[t, dy, j], r_y.at[t, dy, j], row, 2 * ys[dy] + core)

    def share_copy(t, dy, cc):
        slot = slabs.at[t, rows_at(ys[(NY - dy) % NY]), half_at(cc)]
        return remote(slot, slot, s_s.at[t, dy], r_s.at[t, dy], row, sibling)

    def collect(t):
        for i in range(4):
            j = lax.rem(quarter + i, 4)

            @pl.when(4 * core + j != z)
            def _():
                piece_recv(t, j).wait_recv()

            for dy in (2, 1, 3):
                slab_copy(t, dy, j, y).start()
        share_copy(t, 0, core).start()

    def share(t):
        for dy in (1, 3, 2):
            for j in range(4):
                slab_copy(t, dy, j, ys[NY - dy]).wait_recv()
            share_copy(t, dy, core).start()
        for dy in (0, 1, 3, 2):
            share_copy(t, dy, 1 - core).wait_recv()

    piece_start(0)
    weight_start(Q)
    piece_start(1)
    for j in range(4):
        gap = slice(PITCH * j + SENT, PITCH * (j + 1))
        for u in (KV, Q, OUT):
            w[u, gap, :] = jnp.zeros((PITCH - SENT, 512), BF16)
        for t in (0, 1):
            slabs[t, gap, :] = jnp.zeros((PITCH - SENT, SUPER), BF16)

    def lane_half(sub):
        return slice(HD * sub, HD * sub + HD)

    def rs_copy(u, sub, step, side):
        to = ls[5 - step] if side == 0 else ls[3 + step]
        return remote(
            part.at[u, to, :, pl.ds(HD * sub, HD)],
            sums.at[u, side, step - 1, :, pl.ds(HD * sub, HD)],
            s_rs.at[u, side, step - 1, sub], r_rs.at[u, side, step - 1, sub], z_row(side), col,
        )

    def rs_step(u, sub, n):
        lanes = lane_half(sub)
        for side in (sub, 1 - sub):
            step = n if side == sub else n + 1
            if step > 4:
                continue
            if n > 1:
                rs_copy(u, sub, step - 1, side).wait_recv()
                to = ls[5 - step] if side == 0 else ls[3 + step]
                part[u, to, :, lanes] = (
                    part[u, to, :, lanes].astype(F32) + sums[u, side, step - 2, :, lanes].astype(F32)
                ).astype(BF16)
            rs_copy(u, sub, step, side).start()

    def rs_both(u, n):
        rs_step(u, 0, n)
        rs_step(u, 1, n)

    def rs_total(u, sub):
        lanes = lane_half(sub)
        rs_copy(u, sub, 4, 1 - sub).wait_recv()
        rs_copy(u, sub, 4, sub).wait_recv()
        return (
            part[u, lz, :, lanes].astype(F32)
            + sums[u, 0, 3, :, lanes].astype(F32)
            + sums[u, 1, 3, :, lanes].astype(F32)
        ).astype(BF16)

    def ag_copy(v, sub, step, side, sending):
        back = step - 1 if sending else step
        slot = ls[(NZ - back) % NZ] if side == 0 else ls[back]
        block = gath.at[v, slot, :, pl.ds(HD * sub, HD)]
        return remote(
            block, block, s_ag.at[v, side, step - 1, sub], r_ag.at[v, side, step - 1, sub],
            z_row(side), col,
        )

    def ag_step(v, sub, n):
        for side in (sub, 1 - sub):
            steps = 4 if side == sub else 3
            if 1 <= n - 1 <= steps:
                ag_copy(v, sub, n - 1, side, False).wait_recv()
            if n <= steps:
                ag_copy(v, sub, n, side, True).start()

    def ag_both(v, n):
        ag_step(v, 0, n)
        ag_step(v, 1, n)

    def gathered(v, h):
        return gath[v, 4 * h : 4 * h + 4].reshape(SUPER, SLAB)

    def gathered_half(v, h, sub):
        return gath[v, 4 * h : 4 * h + 4, :, lane_half(sub)].reshape(SUPER, HD)

    def project(u, t):
        for h in (0, 1):
            part[u, 4 * h : 4 * h + 4] = (
                dot(slabs[t], w[u, :, 256 * h : 256 * h + 256], 0, 0)
                .astype(BF16)
                .reshape(4, SLAB, SLAB)
            )

    collect(0)
    weight_forward(KV)
    weight_forward(Q)
    collect(1)
    weight_start(OUT)
    share(0)
    weight_wait(KV)
    project(KV, 0)
    rs_both(KV, 1)
    weight_wait(Q)
    project(Q, 0)
    rs_both(KV, 2)
    rs_both(Q, 1)
    weight_forward(OUT)
    share(1)
    rs_both(KV, 3)
    rs_both(Q, 2)
    weight_wait(OUT)
    project(OUT, 1)
    rs_both(KV, 4)
    rs_both(Q, 3)
    own_keys = pl.ds(BACK * SLAB, SLAB)

    def kv_copy(i, sub):
        lanes = pl.ds(HD * sub, HD)
        return remote(
            kvwin.at[own_keys, lanes], kvwin.at[pl.ds((BACK - i) * SLAB, SLAB), lanes],
            s_kv.at[i - 1, sub], r_kv.at[i - 1, sub], token_row(i), col,
        )

    for sub in (0, 1):
        kvwin[own_keys, lane_half(sub)] = rs_total(KV, sub)
        for i in (3, 2, 1, 4):
            kv_copy(i, sub).start()
    rs_both(Q, 4)
    rs_both(OUT, 1)

    def scale_of(values):
        return lax.rsqrt(jnp.mean(values * values, axis=-1, keepdims=True) + epsilon)

    qgain = qg_ref[...] * query_scalar ** (-0.5)
    kgain = kg_ref[...]

    def key_block(s):
        rows = slice(s * SLAB, s * SLAB + SLAB)
        k = kvwin[rows, 0:HD].astype(F32)
        kh[rows, :] = (k * scale_of(k) * kgain).astype(BF16)

    key_block(BACK)
    for r in range(2):
        q_raw[:, lane_half(r)] = rs_total(Q, r)
        q = q_raw[:, lane_half(r)].astype(F32)
        qh[SLAB * r : SLAB * r + SLAB, :] = (q * scale_of(q) * qgain).astype(BF16)

    def score_block(s):
        rows = slice(s * SLAB, s * SLAB + SLAB)
        scores[:, rows] = dot(qh[...], kh[rows, :], 1, 1)

    score_block(BACK)
    rs_both(OUT, 2)
    for i in (1, 4, 2, 3):
        kv_copy(i, 0).wait_recv()
        key_block(BACK - i)
        score_block(BACK - i)
    rs_both(OUT, 3)
    chunk = 32
    first_key = WINDOW - SLAB * place_in_ring

    def softmax(n):
        rows = pl.ds(pl.multiple_of(n * chunk, chunk), chunk)
        t0 = lax.rem(n, SLAB // chunk) * chunk
        t = t0 + lax.broadcasted_iota(jnp.int32, (chunk, 1), 0)
        key = lax.broadcasted_iota(jnp.int32, (chunk, KEYS), 1)
        allowed = (key <= t + WINDOW) & (key >= jnp.maximum(t + 1, first_key))
        s = jnp.where(allowed, scores[rows, :], -1e30)
        e = jnp.exp(s - jnp.max(s, axis=-1, keepdims=True))
        pb[rows, :] = (e * (1.0 / jnp.sum(e, axis=-1, keepdims=True))).astype(BF16)

    pl.loop(0, SLAB // chunk)(softmax)
    rs_both(OUT, 4)
    pl.loop(SLAB // chunk, 2 * SLAB // chunk)(softmax)
    for i in range(1, BACK + 1):
        kv_copy(i, 1).wait_recv()

    def dk_copy(i, sub):
        lanes = pl.ds(HD * sub, HD)
        return remote(
            dkv.at[BACK - i, :, lanes], dkv_in.at[i - 1, :, lanes],
            s_dk.at[i - 1, sub], r_dk.at[i - 1, sub], token_row(-i), col,
        )

    def owned(sub):
        for i in range(1, BACK + 1):
            dk_copy(i, sub).wait_recv()
        total = dkv_own[:, lane_half(sub)]
        for i in range(BACK):
            total = total + dkv_in[i, :, lane_half(sub)].astype(F32)
        gath[DKV, lz, :, lane_half(sub)] = total.astype(BF16)

    for r in range(2):
        datt[SLAB * r : SLAB * r + SLAB, :] = rs_total(OUT, r)
    dvh = dot(pb[...], datt[...], 0, 0)
    dkv_own[:, HD:] = dvh[BACK * SLAB :]
    for s in range(BACK):
        dkv[s, :, HD:] = dvh[s * SLAB : s * SLAB + SLAB].astype(BF16)
    for i in (3, 2, 1, 4):
        dk_copy(i, 1).start()

    blended = dot(pb[...], kvwin[:, HD:], 1, 0).astype(BF16)
    for r in range(2):
        gath[ATT, lz, :, lane_half(r)] = blended[SLAB * r : SLAB * r + SLAB]
    ag_both(ATT, 1)
    scores[...] = dot(datt[...], kvwin[:, HD:], 1, 1)

    def softmax_back(n):
        rows = pl.ds(pl.multiple_of(n * chunk, chunk), chunk)
        p = pb[rows, :].astype(F32)
        dp = scores[rows, :]
        delta = jnp.sum(p * dp, axis=-1, keepdims=True)
        ds[rows, :] = (p * (dp - delta)).astype(BF16)

    pl.loop(0, 2 * SLAB // chunk)(softmax_back)

    def norm_back(raw, gain, grad):
        r = scale_of(raw)
        inner = grad * gain
        return r * inner - raw * (r * r * r * jnp.mean(raw * inner, axis=-1, keepdims=True))

    dkh = dot(ds[...], qh[...], 0, 0)
    for s in range(BACK + 1):
        rows = slice(s * SLAB, s * SLAB + SLAB)
        dk = norm_back(kvwin[rows, 0:HD].astype(F32), kgain, dkh[rows])
        if s == BACK:
            dkv_own[:, 0:HD] = dk
        else:
            dkv[s, :, 0:HD] = dk.astype(BF16)
    for i in (3, 2, 1, 4):
        dk_copy(i, 0).start()
    ag_both(ATT, 2)
    owned(1)
    ag_step(DKV, 1, 1)

    dqh = dot(ds[...], kh[...], 1, 0)
    for r in range(2):
        gath[DQ, lz, :, lane_half(r)] = norm_back(
            q_raw[:, lane_half(r)].astype(F32), qgain, dqh[SLAB * r : SLAB * r + SLAB]
        ).astype(BF16)
    ag_both(DQ, 1)
    ag_both(ATT, 3)
    ag_step(DKV, 1, 2)

    def rl_copy(u, side):
        return remote(
            g.at[u, rows_at(xs[2]), pl.ds(256 * side, 256)], relay.at[u, side],
            s_rl.at[u, side], r_rl.at[u, side], x_row(side), col,
        )

    def fl_copy(u, side):
        return remote(
            g.at[u, rows_at(xs[1] if side == 0 else xs[3])], full.at[u, side],
            s_fl.at[u, side], r_fl.at[u, side], x_row(side), col,
        )

    def grad_start(u, t, v):
        for h in (0, 1):
            g[u, :, 256 * h : 256 * h + 256] = dot(slabs[t], gathered(v, h), 1, 0).astype(BF16)
        rl_copy(u, 0).start()
        rl_copy(u, 1).start()

    def grad_middle(u):
        for side in (0, 1):
            rl_copy(u, side).wait_recv()
            rows = rows_at(xs[1] if side == 0 else xs[3])
            lanes = slice(256 * side, 256 * side + 256)
            g[u, rows, lanes] = (
                g[u, rows, lanes].astype(F32) + relay[u, side].astype(F32)
            ).astype(BF16)
            fl_copy(u, side).start()

    def grad_last(u):
        fl_copy(u, 0).wait_recv()
        fl_copy(u, 1).wait_recv()
        total = (
            g[u, own_rows, :].astype(F32)
            + full[u, 0].astype(F32)
            + full[u, 1].astype(F32)
        ).astype(BF16)
        return total[0:OWN]

    def os_copy(t, dy, cc):
        return remote(
            ypart.at[t, rows_at(ys[dy]), half_at(1 - cc)], ysib.at[t, dy],
            s_os.at[t, dy], r_os.at[t, dy], row, sibling,
        )

    def oy_copy(t, dy):
        return remote(
            ypart.at[t, rows_at(ys[dy]), half_at(core)], yrecv.at[t, dy - 1],
            s_oy.at[t, dy], r_oy.at[t, dy], row, 2 * ys[dy] + core,
        )

    def oz_copy(t, j):
        return remote(
            ypart.at[t, rows_at(y), lanes_at(4 * core + j)], last.at[t, rows_at(quarter)],
            s_oz.at[t, j], r_oz.at[t, quarter], x * NZ + 4 * core + j, 2 * y + head,
        )

    def oz_recv(t, j):
        slot = last.at[t, pl.ds(PITCH * j, SENT)]
        return remote(
            slot, slot, s_oz.at[t, j], r_oz.at[t, j], x * NZ + 4 * core + j, 2 * y + head
        )

    def out_start(t):
        for dy in (2, 1, 3, 0):
            os_copy(t, dy, core).start()

    def out_middle(t):
        for dy in (2, 1, 3, 0):
            os_copy(t, dy, core).wait_recv()
            rows, lanes = rows_at(ys[dy]), half_at(core)
            ypart[t, rows, lanes] = (
                ypart[t, rows, lanes].astype(F32) + ysib[t, dy].astype(F32)
            ).astype(BF16)
            if dy:
                oy_copy(t, dy).start()

    def out_sum(t):
        for dy in (1, 3, 2):
            oy_copy(t, dy).wait_recv()
        rows, lanes = rows_at(y), half_at(core)
        total = ypart[t, rows, lanes].astype(F32)
        for dy in (1, 2, 3):
            total = total + yrecv[t, dy - 1].astype(F32)
        ypart[t, rows, lanes] = total.astype(BF16)
        for j in range(4):
            @pl.when(4 * core + j != z)
            def _():
                oz_copy(t, j).start()

            @pl.when(4 * core + j == z)
            def _():
                last[t, PITCH * j : PITCH * j + SENT] = ypart[t, rows, lanes_at(z)]

    def out_last(t, out):
        for j in range(4):
            @pl.when(4 * core + j != z)
            def _():
                oz_recv(t, j).wait_recv()
        for j in range(4):
            out[OWN * j : OWN * j + OWN] = last[t, PITCH * j : PITCH * j + OWN]

    owned(0)
    ag_step(DKV, 0, 1)
    ag_both(ATT, 4)
    ag_both(DQ, 2)
    ag_step(DKV, 0, 2)
    ag_step(DKV, 1, 3)
    ag_both(ATT, 5)
    grad_start(OUT, 1, ATT)
    ag_step(DKV, 0, 3)
    ag_both(DQ, 3)
    ag_step(DKV, 1, 4)
    ypart[0] = (
        dot(w[OUT, :, 0:256], gathered(ATT, 0), 1, 1)
        + dot(w[OUT, :, 256:512], gathered(ATT, 1), 1, 1)
    ).astype(BF16)
    out_start(0)
    ag_step(DKV, 0, 4)
    ag_both(DQ, 4)
    grad_middle(OUT)
    out_middle(0)
    ag_step(DKV, 1, 5)
    ag_both(DQ, 5)
    rest[...] = (
        dot(w[Q, :, 0:256], gathered(DQ, 0), 1, 1)
        + dot(w[Q, :, 256:512], gathered(DQ, 1), 1, 1)
        + dot(w[KV, :, 128:256], gathered_half(DKV, 0, 1), 1, 1)
        + dot(w[KV, :, 384:512], gathered_half(DKV, 1, 1), 1, 1)
    )
    ag_step(DKV, 0, 5)
    for dy in (2, 1, 3, 0):
        rows = pl.ds(pl.multiple_of(PITCH * ys[dy], 16), PITCH)
        ypart[1, rows, :] = (
            rest[rows, :]
            + dot(w[KV, rows, 0:128], gathered_half(DKV, 0, 0), 1, 1)
            + dot(w[KV, rows, 256:384], gathered_half(DKV, 1, 0), 1, 1)
        ).astype(BF16)
        os_copy(1, dy, core).start()
    out_middle(1)
    grad_start(Q, 0, DQ)
    grad_start(KV, 0, DKV)
    grad_middle(Q)
    grad_middle(KV)
    out_sum(0)
    go_out[...] = grad_last(OUT)
    out_sum(1)
    gq_out[...] = grad_last(Q)
    done = grad_last(KV)
    for h in (0, 1):
        gk_out[:, 128 * h : 128 * h + 128] = done[:, 256 * h : 256 * h + 128]
        gv_out[:, 128 * h : 128 * h + 128] = done[:, 256 * h + 128 : 256 * h + 256]
    out_last(0, layer_out)
    out_last(1, input_grad)

    for u in (KV, Q, OUT):
        for side in (0, 1):
            xf_copy(u, side, x).wait_send()
            xh_copy(u, side, xs[3] if side == 0 else xs[1]).wait_send()
            rl_copy(u, side).wait_send()
            fl_copy(u, side).wait_send()
            for sub in (0, 1):
                for step in range(1, 5):
                    if step > 1 or side == sub:
                        rs_copy(u, sub, step, side).wait_send()
                    if step < 4 or side == sub:
                        ag_copy(u, sub, step, side, True).wait_send()
    for t in (0, 1):
        for j in range(4):
            @pl.when(4 * core + j != z)
            def _():
                piece_copy(t, j).wait_send()
                oz_copy(t, j).wait_send()
        for dy in range(NY):
            share_copy(t, dy, core).wait_send()
            os_copy(t, dy, core).wait_send()
            if dy:
                for j in range(4):
                    slab_copy(t, dy, j, y).wait_send()
                oy_copy(t, dy).wait_send()

    for i in range(1, BACK + 1):
        for sub in (0, 1):
            kv_copy(i, sub).wait_send()
            dk_copy(i, sub).wait_send()


def hand_over(*refs):
    for source, target in zip(refs[:6], refs[6:]):
        target[...] = source[...]


def shards(tokens, w_query, w_key, w_value, w_output, query_gain, key_gain, cotangent):
    vmem = lambda *shape, dtype=BF16: pltpu.VMEM(shape, dtype)
    dma = lambda *shape: pltpu.SemaphoreType.DMA(shape)
    spec = pl.BlockSpec(memory_space=pltpu.VMEM)
    scratch = [
        vmem(2, BLOCK, TOK), vmem(2, BLOCK, SUPER),
        vmem(3, BLOCK, 512), vmem(3, BLOCK, 512),
        vmem(3, NZ, SLAB, SLAB), vmem(3, 2, 4, SLAB, SLAB),
        vmem(3, NZ, SLAB, SLAB),
        vmem(SLAB, SLAB), vmem(2 * SLAB, HD), vmem(KEYS, HD), vmem(KEYS, 2 * HD),
        vmem(2 * SLAB, KEYS, dtype=F32), vmem(2 * SLAB, KEYS), vmem(2 * SLAB, KEYS),
        vmem(2 * SLAB, HD),
        vmem(BACK, SLAB, 256), vmem(SLAB, 256, dtype=F32), vmem(BACK, SLAB, 256),
        vmem(2, BLOCK, SUPER), vmem(BLOCK, SUPER, dtype=F32),
        vmem(2, NY, SENT, 512), vmem(2, 3, SENT, 512),
        vmem(2, BLOCK, TOK), vmem(3, 2, SENT, 256), vmem(3, 2, SENT, 512),
        dma(3, 2), dma(3, 2), dma(3, 2), dma(3, 2),
        dma(2, 4), dma(2, 4), dma(2, NY, 4), dma(2, NY, 4), dma(2, NY), dma(2, NY),
        dma(3, 2, 4, 2), dma(3, 2, 4, 2), dma(3, 2, 4, 2), dma(3, 2, 4, 2),
        dma(BACK, 2), dma(BACK, 2), dma(BACK, 2), dma(BACK, 2),
        dma(3, 2), dma(3, 2), dma(3, 2), dma(3, 2),
        dma(2, NY), dma(2, NY), dma(2, NY), dma(2, NY), dma(2, 4), dma(2, 4),
    ]
    outs = [
        jax.ShapeDtypeStruct(tokens.shape[::-1], BF16),
        jax.ShapeDtypeStruct(tokens.shape[::-1], BF16),
        jax.ShapeDtypeStruct(w_query.shape, BF16),
        jax.ShapeDtypeStruct(w_key.shape, BF16),
        jax.ShapeDtypeStruct(w_value.shape, BF16),
        jax.ShapeDtypeStruct(w_output.shape[::-1], BF16),
    ]
    results = pl.pallas_call(
        kernel,
        out_shape=outs,
        in_specs=[spec] * 8,
        out_specs=[spec] * 6,
        scratch_shapes=scratch,
        compiler_params=pltpu.CompilerParams(
            collective_id=0, has_side_effects=True, vmem_limit_bytes=60 * 1024 * 1024
        ),
    )(
        tokens.T, cotangent.T, w_query, w_key, w_value, w_output.T,
        query_gain.reshape(1, HD), key_gain.reshape(1, HD),
    )
    layer_out, input_grad, gq, gk, gv, go = pl.pallas_call(
        hand_over, out_shape=outs, in_specs=[spec] * 6, out_specs=[spec] * 6
    )(*results)
    return layer_out.T, input_grad.T, gq, gk, gv, go.T


def solution(mesh):
    in_specs = (
        P("row", "col"), P("row", "col"), P("row", "col"), P("row", "col"), P("col", "row"),
        P(), P(), P("row", "col"),
    )
    out_specs = (
        P("row", "col"), P("row", "col"), P("row", "col"), P("row", "col"), P("row", "col"),
        P("col", "row"),
    )
    return jax.shard_map(shards, mesh=mesh, in_specs=in_specs, out_specs=out_specs, check_vma=False)
```

```python
import jax
import jax.numpy as jnp
from jax import lax
from jax.experimental import pallas as pl
from jax.experimental.pallas import tpu as pltpu
from jax.sharding import PartitionSpec as P

BF16 = jnp.bfloat16
F32 = jnp.float32

NX, NZ, NY = 4, 8, 4

OWN, SENT, PITCH, BLOCK = 168, 176, 192, 768
TOK = 128
SUPER = 1024
SLAB = 256
HD = 128
BACK = 4
KEYS = (BACK + 1) * SLAB
WINDOW = 1024
KV, Q, OUT = 0, 1, 2
ATT, DQ, DKV = 0, 1, 2
query_scalar = 168.0
epsilon = 1e-06


def dot(a, b, ca, cb):
    return lax.dot_general(a, b, (((ca,), (cb,)), ((), ())), preferred_element_type=F32)


def ring(a, n):
    return lax.rem(a + n, n)


def kernel(
    tok_in, cot_in, wq_in, wk_in, wv_in, wo_in, qg_ref, kg_ref,
    layer_out, input_grad, gq_out, gk_out, gv_out, go_out,
    piece, slabs, w, g, part, sums, gath,
    q_raw, qh, kh, kvwin, scores, pb, ds, datt, dkv, dkv_own, dkv_in,
    ypart, rest, ysib, yrecv, last, relay, full,
    s_xf, r_xf, s_xh, r_xh, s_p, r_p, s_y, r_y, s_s, r_s,
    s_rs, r_rs, s_ag, r_ag, s_kv, r_kv, s_dk, r_dk,
    s_rl, r_rl, s_fl, r_fl, s_os, r_os, s_oy, r_oy, s_oz, r_oz,
):
    row = lax.axis_index("row")
    col = lax.axis_index("col")
    x, z = lax.div(row, NZ), lax.rem(row, NZ)
    y, core = lax.div(col, 2), lax.rem(col, 2)
    head, quarter = lax.div(z, 4), lax.rem(z, 4)
    xs = [ring(x + d, NX) for d in range(NX)]
    zs = [ring(z + d, NZ) for d in range(NZ)]
    ys = [ring(y + d, NY) for d in range(NY)]
    sibling = col + 1 - 2 * core
    shift = 2 * core
    ls = [ring(z + shift + d, NZ) for d in range(NZ)]
    lz = ls[0]
    place_in_ring = 4 * x + lax.rem(lz, 4)

    def remote(src, dst, ssem, rsem, to_row, to_col):
        return pltpu.make_async_remote_copy(
            src_ref=src, dst_ref=dst, send_sem=ssem, recv_sem=rsem,
            device_id={"row": to_row, "col": to_col}, device_id_type=pl.DeviceIdType.MESH,
        )

    def token_row(i):
        at = lax.rem(place_in_ring + 16 + i, 16)
        return lax.div(at, 4) * NZ + ring(4 * lax.div(lz, 4) + lax.rem(at, 4) + NZ - shift, NZ)

    def x_row(side):
        return (xs[1] if side == 0 else xs[3]) * NZ + z

    def z_row(side):
        return x * NZ + (zs[1] if side == 0 else zs[7])

    barrier = pltpu.get_barrier_semaphore()

    def greet(to_row, to_col):
        pl.semaphore_signal(
            barrier, inc=1, device_id={"row": to_row, "col": to_col},
            device_id_type=pl.DeviceIdType.MESH,
        )

    at_home = core == head
    for j in range(4):
        @pl.when(4 * core + j != z)
        def _():
            greet(x * NZ + 4 * core + j, 2 * y + head)

    greet(z_row(0), col)
    greet(z_row(1), col)
    for d in range(1, NY):
        greet(row, 2 * ys[d] + core)
    for i in range(1, BACK + 1):
        greet(token_row(i), col)
        greet(token_row(-i), col)
    greet(row, sibling)
    greet(x_row(0), col)
    greet(x_row(1), col)

    def rows_at(i):
        return pl.ds(pl.multiple_of(PITCH * i, 16), SENT)

    own_rows = rows_at(x)
    for u in (KV, Q, OUT):
        w[u, pl.ds(pl.multiple_of(PITCH * x + 160, 16), 16), :] = jnp.zeros((16, 512), BF16)
    weight_rows = pl.ds(pl.multiple_of(PITCH * x, 16), OWN)
    for h in (0, 1):
        w[KV, weight_rows, 256 * h : 256 * h + 128] = wk_in[:, 128 * h : 128 * h + 128]
        w[KV, weight_rows, 256 * h + 128 : 256 * h + 256] = wv_in[:, 128 * h : 128 * h + 128]
    w[Q, weight_rows, :] = wq_in[...]
    w[OUT, weight_rows, :] = wo_in[...]

    for t, src in ((0, tok_in), (1, cot_in)):
        for j in range(4):
            piece[t, PITCH * j + 160 : PITCH * j + SENT] = jnp.zeros((SENT - 160, TOK), BF16)
            piece[t, PITCH * j : PITCH * j + OWN] = src[OWN * j : OWN * j + OWN]

    pl.semaphore_wait(barrier, 20 - at_home.astype(jnp.int32))

    def xf_copy(u, side, xx):
        slot = w.at[u, rows_at(xx)]
        return remote(slot, slot, s_xf.at[u, side], r_xf.at[u, side], x_row(side), col)

    def xh_copy(u, side, xx):
        slot = w.at[u, rows_at(xx), pl.ds(256 * side, 256)]
        return remote(slot, slot, s_xh.at[u, side], r_xh.at[u, side], x_row(side), col)

    def weight_start(u):
        xf_copy(u, 0, x).start()
        xf_copy(u, 1, x).start()

    def weight_forward(u):
        xf_copy(u, 0, xs[3]).wait_recv()
        xh_copy(u, 0, xs[3]).start()
        xf_copy(u, 1, xs[1]).wait_recv()
        xh_copy(u, 1, xs[1]).start()

    def weight_wait(u):
        xh_copy(u, 0, xs[2]).wait_recv()
        xh_copy(u, 1, xs[2]).wait_recv()

    weight_start(KV)

    def lanes_at(i):
        return pl.ds(pl.multiple_of(TOK * i, TOK), TOK)

    def half_at(c):
        return pl.ds(pl.multiple_of(512 * c, 512), 512)

    def piece_copy(t, j):
        return remote(
            piece.at[t, pl.ds(PITCH * j, SENT)], slabs.at[t, rows_at(y), lanes_at(z)],
            s_p.at[t, j], r_p.at[t, quarter], x * NZ + 4 * core + j, 2 * y + head,
        )

    def piece_recv(t, j):
        slot = slabs.at[t, rows_at(y), lanes_at(4 * core + j)]
        return remote(
            slot, slot, s_p.at[t, 0], r_p.at[t, j], x * NZ + 4 * core + j, 2 * y + head
        )

    def piece_start(t):
        for j in range(4):
            @pl.when(4 * core + j != z)
            def _():
                piece_copy(t, j).start()

            @pl.when(4 * core + j == z)
            def _():
                slabs[t, rows_at(y), lanes_at(z)] = piece[t, PITCH * j : PITCH * j + SENT]

    def slab_copy(t, dy, j, yy):
        slot = slabs.at[t, rows_at(yy), lanes_at(4 * core + j)]
        return remote(slot, slot, s_y.at[t, dy, j], r_y.at[t, dy, j], row, 2 * ys[dy] + core)

    def share_copy(t, dy, cc):
        slot = slabs.at[t, rows_at(ys[(NY - dy) % NY]), half_at(cc)]
        return remote(slot, slot, s_s.at[t, dy], r_s.at[t, dy], row, sibling)

    def collect(t):
        for i in range(4):
            j = lax.rem(quarter + i, 4)

            @pl.when(4 * core + j != z)
            def _():
                piece_recv(t, j).wait_recv()

            for dy in (2, 1, 3):
                slab_copy(t, dy, j, y).start()
        share_copy(t, 0, core).start()

    def share(t):
        for dy in (1, 3, 2):
            for j in range(4):
                slab_copy(t, dy, j, ys[NY - dy]).wait_recv()
            share_copy(t, dy, core).start()
        for dy in (0, 1, 3, 2):
            share_copy(t, dy, 1 - core).wait_recv()

    piece_start(0)
    weight_start(Q)
    piece_start(1)
    for j in range(4):
        gap = slice(PITCH * j + SENT, PITCH * (j + 1))
        for u in (KV, Q, OUT):
            w[u, gap, :] = jnp.zeros((PITCH - SENT, 512), BF16)
        for t in (0, 1):
            slabs[t, gap, :] = jnp.zeros((PITCH - SENT, SUPER), BF16)

    def lane_half(sub):
        return slice(HD * sub, HD * sub + HD)

    def rs_copy(u, sub, step, side):
        to = ls[5 - step] if side == 0 else ls[3 + step]
        return remote(
            part.at[u, to, :, pl.ds(HD * sub, HD)],
            sums.at[u, side, step - 1, :, pl.ds(HD * sub, HD)],
            s_rs.at[u, side, step - 1, sub], r_rs.at[u, side, step - 1, sub], z_row(side), col,
        )

    def rs_step(u, sub, n):
        lanes = lane_half(sub)
        for side in (sub, 1 - sub):
            step = n if side == sub else n + 1
            if step > 4:
                continue
            if n > 1:
                rs_copy(u, sub, step - 1, side).wait_recv()
                to = ls[5 - step] if side == 0 else ls[3 + step]
                part[u, to, :, lanes] = (
                    part[u, to, :, lanes].astype(F32) + sums[u, side, step - 2, :, lanes].astype(F32)
                ).astype(BF16)
            rs_copy(u, sub, step, side).start()

    def rs_both(u, n):
        rs_step(u, 0, n)
        rs_step(u, 1, n)

    def rs_total(u, sub):
        lanes = lane_half(sub)
        rs_copy(u, sub, 4, 1 - sub).wait_recv()
        rs_copy(u, sub, 4, sub).wait_recv()
        return (
            part[u, lz, :, lanes].astype(F32)
            + sums[u, 0, 3, :, lanes].astype(F32)
            + sums[u, 1, 3, :, lanes].astype(F32)
        ).astype(BF16)

    def ag_copy(v, sub, step, side, sending):
        back = step - 1 if sending else step
        slot = ls[(NZ - back) % NZ] if side == 0 else ls[back]
        block = gath.at[v, slot, :, pl.ds(HD * sub, HD)]
        return remote(
            block, block, s_ag.at[v, side, step - 1, sub], r_ag.at[v, side, step - 1, sub],
            z_row(side), col,
        )

    def ag_step(v, sub, n):
        for side in (sub, 1 - sub):
            steps = 4 if side == sub else 3
            if 1 <= n - 1 <= steps:
                ag_copy(v, sub, n - 1, side, False).wait_recv()
            if n <= steps:
                ag_copy(v, sub, n, side, True).start()

    def ag_both(v, n):
        ag_step(v, 0, n)
        ag_step(v, 1, n)

    def gathered(v, h):
        return gath[v, 4 * h : 4 * h + 4].reshape(SUPER, SLAB)

    def gathered_half(v, h, sub):
        return gath[v, 4 * h : 4 * h + 4, :, lane_half(sub)].reshape(SUPER, HD)

    def project(u, t):
        product = dot(slabs[t], w[u], 0, 0).astype(BF16)
        for h in (0, 1):
            part[u, 4 * h : 4 * h + 4] = product[:, 256 * h : 256 * h + 256].reshape(4, SLAB, SLAB)

    collect(0)
    weight_forward(KV)
    weight_forward(Q)
    collect(1)
    weight_start(OUT)
    share(0)
    weight_wait(KV)
    project(KV, 0)
    rs_both(KV, 1)
    weight_wait(Q)
    project(Q, 0)
    rs_both(KV, 2)
    rs_both(Q, 1)
    weight_forward(OUT)
    share(1)
    rs_both(KV, 3)
    rs_both(Q, 2)
    weight_wait(OUT)
    project(OUT, 1)
    rs_both(KV, 4)
    rs_both(Q, 3)
    rs_both(OUT, 1)
    own_keys = pl.ds(BACK * SLAB, SLAB)

    def kv_copy(i, sub):
        lanes = pl.ds(HD * sub, HD)
        return remote(
            kvwin.at[own_keys, lanes], kvwin.at[pl.ds((BACK - i) * SLAB, SLAB), lanes],
            s_kv.at[i - 1, sub], r_kv.at[i - 1, sub], token_row(i), col,
        )

    for sub in (0, 1):
        kvwin[own_keys, lane_half(sub)] = rs_total(KV, sub)
        for i in (3, 2, 1, 4):
            kv_copy(i, sub).start()
        if sub == 0:
            rs_both(Q, 4)

    def scale_of(values):
        return lax.rsqrt(jnp.mean(values * values, axis=-1, keepdims=True) + epsilon)

    qgain = qg_ref[...] * query_scalar ** (-0.5)
    kgain = kg_ref[...]

    def key_block(s):
        rows = slice(s * SLAB, s * SLAB + SLAB)
        k = kvwin[rows, 0:HD].astype(F32)
        kh[rows, :] = (k * scale_of(k) * kgain).astype(BF16)

    key_block(BACK)
    for r in range(2):
        q_raw[:, lane_half(r)] = rs_total(Q, r)
        q = q_raw[:, lane_half(r)].astype(F32)
        qh[SLAB * r : SLAB * r + SLAB, :] = (q * scale_of(q) * qgain).astype(BF16)

    def score_block(s):
        rows = slice(s * SLAB, s * SLAB + SLAB)
        scores[:, rows] = dot(qh[...], kh[rows, :], 1, 1)

    score_block(BACK)
    rs_both(OUT, 2)
    for i in (1, 4, 2, 3):
        kv_copy(i, 0).wait_recv()
        key_block(BACK - i)
        score_block(BACK - i)
    rs_both(OUT, 3)
    chunk = 64
    first_key = WINDOW - SLAB * place_in_ring

    def softmax(n):
        rows = pl.ds(pl.multiple_of(n * chunk, chunk), chunk)
        t0 = lax.rem(n, SLAB // chunk) * chunk
        t = t0 + lax.broadcasted_iota(jnp.int32, (chunk, 1), 0)
        key = lax.broadcasted_iota(jnp.int32, (chunk, KEYS), 1)
        allowed = (key <= t + WINDOW) & (key >= jnp.maximum(t + 1, first_key))
        s = jnp.where(allowed, scores[rows, :], -1e30)
        e = jnp.exp(s - jnp.max(s, axis=-1, keepdims=True))
        pb[rows, :] = (e * (1.0 / jnp.sum(e, axis=-1, keepdims=True))).astype(BF16)

    pl.loop(0, SLAB // chunk)(softmax)
    rs_both(OUT, 4)
    pl.loop(SLAB // chunk, 2 * SLAB // chunk)(softmax)
    for i in range(1, BACK + 1):
        kv_copy(i, 1).wait_recv()

    def dk_copy(i, sub):
        lanes = pl.ds(HD * sub, HD)
        return remote(
            dkv.at[BACK - i, :, lanes], dkv_in.at[i - 1, :, lanes],
            s_dk.at[i - 1, sub], r_dk.at[i - 1, sub], token_row(-i), col,
        )

    def owned(sub):
        for i in range(1, BACK + 1):
            dk_copy(i, sub).wait_recv()
        total = dkv_own[:, lane_half(sub)]
        for i in range(BACK):
            total = total + dkv_in[i, :, lane_half(sub)].astype(F32)
        gath[DKV, lz, :, lane_half(sub)] = total.astype(BF16)

    blended = dot(pb[...], kvwin[:, HD:], 1, 0).astype(BF16)
    for r in range(2):
        gath[ATT, lz, :, lane_half(r)] = blended[SLAB * r : SLAB * r + SLAB]
    ag_both(ATT, 1)
    for r in range(2):
        datt[SLAB * r : SLAB * r + SLAB, :] = rs_total(OUT, r)
    dvh = dot(pb[...], datt[...], 0, 0)
    dkv_own[:, HD:] = dvh[BACK * SLAB :]
    for s in range(BACK):
        dkv[s, :, HD:] = dvh[s * SLAB : s * SLAB + SLAB].astype(BF16)
    for i in (3, 2, 1, 4):
        dk_copy(i, 1).start()

    scores[...] = dot(datt[...], kvwin[:, HD:], 1, 1)

    def softmax_back(n):
        rows = pl.ds(pl.multiple_of(n * chunk, chunk), chunk)
        p = pb[rows, :].astype(F32)
        dp = scores[rows, :]
        delta = jnp.sum(p * dp, axis=-1, keepdims=True)
        ds[rows, :] = (p * (dp - delta)).astype(BF16)

    pl.loop(0, 2 * SLAB // chunk)(softmax_back)

    def norm_back(raw, gain, grad):
        r = scale_of(raw)
        inner = grad * gain
        return r * inner - raw * (r * r * r * jnp.mean(raw * inner, axis=-1, keepdims=True))

    dkh = dot(ds[...], qh[...], 0, 0)
    for s in range(BACK + 1):
        rows = slice(s * SLAB, s * SLAB + SLAB)
        dk = norm_back(kvwin[rows, 0:HD].astype(F32), kgain, dkh[rows])
        if s == BACK:
            dkv_own[:, 0:HD] = dk
        else:
            dkv[s, :, 0:HD] = dk.astype(BF16)
    for i in (3, 2, 1, 4):
        dk_copy(i, 0).start()
    ag_both(ATT, 2)
    owned(1)
    ag_step(DKV, 1, 1)

    dqh = dot(ds[...], kh[...], 1, 0)
    for r in range(2):
        gath[DQ, lz, :, lane_half(r)] = norm_back(
            q_raw[:, lane_half(r)].astype(F32), qgain, dqh[SLAB * r : SLAB * r + SLAB]
        ).astype(BF16)
    ag_both(DQ, 1)
    ag_both(ATT, 3)
    ag_step(DKV, 1, 2)

    def rl_copy(u, side):
        return remote(
            g.at[u, rows_at(xs[2]), pl.ds(256 * side, 256)], relay.at[u, side],
            s_rl.at[u, side], r_rl.at[u, side], x_row(side), col,
        )

    def fl_copy(u, side):
        return remote(
            g.at[u, rows_at(xs[1] if side == 0 else xs[3])], full.at[u, side],
            s_fl.at[u, side], r_fl.at[u, side], x_row(side), col,
        )

    def grad_start(u, t, v):
        for h in (0, 1):
            g[u, :, 256 * h : 256 * h + 256] = dot(slabs[t], gathered(v, h), 1, 0).astype(BF16)
        rl_copy(u, 0).start()
        rl_copy(u, 1).start()

    def grad_middle(u):
        for side in (0, 1):
            rl_copy(u, side).wait_recv()
            rows = rows_at(xs[1] if side == 0 else xs[3])
            lanes = slice(256 * side, 256 * side + 256)
            g[u, rows, lanes] = (
                g[u, rows, lanes].astype(F32) + relay[u, side].astype(F32)
            ).astype(BF16)
            fl_copy(u, side).start()

    def grad_last(u):
        fl_copy(u, 0).wait_recv()
        fl_copy(u, 1).wait_recv()
        total = (
            g[u, own_rows, :].astype(F32)
            + full[u, 0].astype(F32)
            + full[u, 1].astype(F32)
        ).astype(BF16)
        return total[0:OWN]

    def os_copy(t, dy, cc):
        return remote(
            ypart.at[t, rows_at(ys[dy]), half_at(1 - cc)], ysib.at[t, dy],
            s_os.at[t, dy], r_os.at[t, dy], row, sibling,
        )

    def oy_copy(t, dy, j):
        return remote(
            ypart.at[t, rows_at(ys[dy]), lanes_at(4 * core + j)],
            yrecv.at[t, dy - 1, :, pl.ds(TOK * j, TOK)],
            s_oy.at[t, dy, j], r_oy.at[t, dy, j], row, 2 * ys[dy] + core,
        )

    def oz_copy(t, j):
        return remote(
            ypart.at[t, rows_at(y), lanes_at(4 * core + j)], last.at[t, rows_at(quarter)],
            s_oz.at[t, j], r_oz.at[t, quarter], x * NZ + 4 * core + j, 2 * y + head,
        )

    def oz_recv(t, j):
        slot = last.at[t, pl.ds(PITCH * j, SENT)]
        return remote(
            slot, slot, s_oz.at[t, j], r_oz.at[t, j], x * NZ + 4 * core + j, 2 * y + head
        )

    def out_start(t):
        for dy in (2, 1, 3, 0):
            os_copy(t, dy, core).start()

    def out_middle(t):
        for dy in (2, 1, 3, 0):
            os_copy(t, dy, core).wait_recv()
            rows, lanes = rows_at(ys[dy]), half_at(core)
            ypart[t, rows, lanes] = (
                ypart[t, rows, lanes].astype(F32) + ysib[t, dy].astype(F32)
            ).astype(BF16)
            if dy == 2:
                for j in range(4):
                    oy_copy(t, 2, j).start()
            if dy == 3:
                for j in range(4):
                    oy_copy(t, 1, j).start()
                    oy_copy(t, 3, j).start()

    def out_sum(t):
        rows = rows_at(y)
        for j in range(4):
            lanes = lanes_at(4 * core + j)
            total = ypart[t, rows, lanes].astype(F32)
            for dy in (2, 1, 3):
                oy_copy(t, dy, j).wait_recv()
                total = total + yrecv[t, dy - 1, :, TOK * j : TOK * j + TOK].astype(F32)
            ypart[t, rows, lanes] = total.astype(BF16)

            @pl.when(4 * core + j != z)
            def _():
                oz_copy(t, j).start()

            @pl.when(4 * core + j == z)
            def _():
                last[t, PITCH * j : PITCH * j + SENT] = total.astype(BF16)

    def out_last(t, out):
        for j in range(4):
            @pl.when(4 * core + j != z)
            def _():
                oz_recv(t, j).wait_recv()
        for j in range(4):
            out[OWN * j : OWN * j + OWN] = last[t, PITCH * j : PITCH * j + OWN]

    owned(0)
    ag_step(DKV, 0, 1)
    ag_both(ATT, 4)
    ag_both(DQ, 2)
    ag_step(DKV, 0, 2)
    ag_step(DKV, 1, 3)
    ag_both(ATT, 5)
    grad_start(OUT, 1, ATT)
    ag_step(DKV, 0, 3)
    ag_both(DQ, 3)
    ag_step(DKV, 1, 4)
    ypart[0] = (
        dot(w[OUT, :, 0:256], gathered(ATT, 0), 1, 1)
        + dot(w[OUT, :, 256:512], gathered(ATT, 1), 1, 1)
    ).astype(BF16)
    out_start(0)
    ag_step(DKV, 0, 4)
    ag_both(DQ, 4)
    grad_middle(OUT)
    out_middle(0)
    ag_step(DKV, 1, 5)
    ag_both(DQ, 5)
    rest[...] = (
        dot(w[Q, :, 0:256], gathered(DQ, 0), 1, 1)
        + dot(w[Q, :, 256:512], gathered(DQ, 1), 1, 1)
        + dot(w[KV, :, 128:256], gathered_half(DKV, 0, 1), 1, 1)
        + dot(w[KV, :, 384:512], gathered_half(DKV, 1, 1), 1, 1)
    )
    grad_start(Q, 0, DQ)
    ag_step(DKV, 0, 5)
    for dy in (2, 1, 3, 0):
        rows = pl.ds(pl.multiple_of(PITCH * ys[dy], 16), PITCH)
        ypart[1, rows, :] = (
            rest[rows, :]
            + dot(w[KV, rows, 0:128], gathered_half(DKV, 0, 0), 1, 1)
            + dot(w[KV, rows, 256:384], gathered_half(DKV, 1, 0), 1, 1)
        ).astype(BF16)
        os_copy(1, dy, core).start()
    out_middle(1)
    grad_start(KV, 0, DKV)
    grad_middle(Q)
    grad_middle(KV)
    out_sum(0)
    go_out[...] = grad_last(OUT)
    out_sum(1)
    gq_out[...] = grad_last(Q)
    done = grad_last(KV)
    for h in (0, 1):
        gk_out[:, 128 * h : 128 * h + 128] = done[:, 256 * h : 256 * h + 128]
        gv_out[:, 128 * h : 128 * h + 128] = done[:, 256 * h + 128 : 256 * h + 256]
    out_last(0, layer_out)
    out_last(1, input_grad)

    for u in (KV, Q, OUT):
        for side in (0, 1):
            xf_copy(u, side, x).wait_send()
            xh_copy(u, side, xs[3] if side == 0 else xs[1]).wait_send()
            rl_copy(u, side).wait_send()
            fl_copy(u, side).wait_send()
            for sub in (0, 1):
                for step in range(1, 5):
                    if step > 1 or side == sub:
                        rs_copy(u, sub, step, side).wait_send()
                    if step < 4 or side == sub:
                        ag_copy(u, sub, step, side, True).wait_send()
    for t in (0, 1):
        for j in range(4):
            @pl.when(4 * core + j != z)
            def _():
                piece_copy(t, j).wait_send()
                oz_copy(t, j).wait_send()
        for dy in range(NY):
            share_copy(t, dy, core).wait_send()
            os_copy(t, dy, core).wait_send()
            if dy:
                for j in range(4):
                    slab_copy(t, dy, j, y).wait_send()
                    oy_copy(t, dy, j).wait_send()

    for i in range(1, BACK + 1):
        for sub in (0, 1):
            kv_copy(i, sub).wait_send()
            dk_copy(i, sub).wait_send()


def hand_over(*refs):
    for source, target in zip(refs[:6], refs[6:]):
        target[...] = source[...]


def shards(tokens, w_query, w_key, w_value, w_output, query_gain, key_gain, cotangent):
    vmem = lambda *shape, dtype=BF16: pltpu.VMEM(shape, dtype)
    dma = lambda *shape: pltpu.SemaphoreType.DMA(shape)
    spec = pl.BlockSpec(memory_space=pltpu.VMEM)
    scratch = [
        vmem(2, BLOCK, TOK), vmem(2, BLOCK, SUPER),
        vmem(3, BLOCK, 512), vmem(3, BLOCK, 512),
        vmem(3, NZ, SLAB, SLAB), vmem(3, 2, 4, SLAB, SLAB),
        vmem(3, NZ, SLAB, SLAB),
        vmem(SLAB, SLAB), vmem(2 * SLAB, HD), vmem(KEYS, HD), vmem(KEYS, 2 * HD),
        vmem(2 * SLAB, KEYS, dtype=F32), vmem(2 * SLAB, KEYS), vmem(2 * SLAB, KEYS),
        vmem(2 * SLAB, HD),
        vmem(BACK, SLAB, 256), vmem(SLAB, 256, dtype=F32), vmem(BACK, SLAB, 256),
        vmem(2, BLOCK, SUPER), vmem(BLOCK, SUPER, dtype=F32),
        vmem(2, NY, SENT, 512), vmem(2, 3, SENT, 512),
        vmem(2, BLOCK, TOK), vmem(3, 2, SENT, 256), vmem(3, 2, SENT, 512),
        dma(3, 2), dma(3, 2), dma(3, 2), dma(3, 2),
        dma(2, 4), dma(2, 4), dma(2, NY, 4), dma(2, NY, 4), dma(2, NY), dma(2, NY),
        dma(3, 2, 4, 2), dma(3, 2, 4, 2), dma(3, 2, 4, 2), dma(3, 2, 4, 2),
        dma(BACK, 2), dma(BACK, 2), dma(BACK, 2), dma(BACK, 2),
        dma(3, 2), dma(3, 2), dma(3, 2), dma(3, 2),
        dma(2, NY), dma(2, NY), dma(2, NY, 4), dma(2, NY, 4), dma(2, 4), dma(2, 4),
    ]
    outs = [
        jax.ShapeDtypeStruct(tokens.shape[::-1], BF16),
        jax.ShapeDtypeStruct(tokens.shape[::-1], BF16),
        jax.ShapeDtypeStruct(w_query.shape, BF16),
        jax.ShapeDtypeStruct(w_key.shape, BF16),
        jax.ShapeDtypeStruct(w_value.shape, BF16),
        jax.ShapeDtypeStruct(w_output.shape[::-1], BF16),
    ]
    results = pl.pallas_call(
        kernel,
        out_shape=outs,
        in_specs=[spec] * 8,
        out_specs=[spec] * 6,
        scratch_shapes=scratch,
        compiler_params=pltpu.CompilerParams(
            collective_id=0, has_side_effects=True, vmem_limit_bytes=60 * 1024 * 1024
        ),
    )(
        tokens.T, cotangent.T, w_query, w_key, w_value, w_output.T,
        query_gain.reshape(1, HD), key_gain.reshape(1, HD),
    )
    layer_out, input_grad, gq, gk, gv, go = pl.pallas_call(
        hand_over, out_shape=outs, in_specs=[spec] * 6, out_specs=[spec] * 6
    )(*results)
    return layer_out.T, input_grad.T, gq, gk, gv, go.T


def solution(mesh):
    in_specs = (
        P("row", "col"), P("row", "col"), P("row", "col"), P("row", "col"), P("col", "row"),
        P(), P(), P("row", "col"),
    )
    out_specs = (
        P("row", "col"), P("row", "col"), P("row", "col"), P("row", "col"), P("row", "col"),
        P("col", "row"),
    )
    return jax.shard_map(shards, mesh=mesh, in_specs=in_specs, out_specs=out_specs, check_vma=False)
```

```python
import jax
import jax.numpy as jnp
from jax import lax
from jax.experimental import pallas as pl
from jax.experimental.pallas import tpu as pltpu
from jax.sharding import PartitionSpec as P

BF16 = jnp.bfloat16
F32 = jnp.float32

NX, NZ, NY = 4, 8, 4

OWN, SENT, PITCH, BLOCK = 168, 176, 192, 768
TOK = 128
SUPER = 1024
SLAB = 256
HD = 128
BACK = 4
KEYS = (BACK + 1) * SLAB
WINDOW = 1024
KV, Q, OUT = 0, 1, 2
ATT, DQ, DKV = 0, 1, 2
query_scalar = 168.0
epsilon = 1e-06


def dot(a, b, ca, cb):
    return lax.dot_general(a, b, (((ca,), (cb,)), ((), ())), preferred_element_type=F32)


def ring(a, n):
    return lax.rem(a + n, n)


def kernel(
    tok_in, cot_in, wq_in, wk_in, wv_in, wo_in, qg_ref, kg_ref,
    layer_out, input_grad, gq_out, gk_out, gv_out, go_out,
    piece, slabs, w, g, part, sums, gath,
    q_raw, qh, kh, kvwin, scores, pb, ds, datt, dkv, dkv_own, dkv_in,
    ypart, rest, ysib, yrecv, last, relay, full,
    s_xf, r_xf, s_xh, r_xh, s_p, r_p, s_y, r_y, s_s, r_s,
    s_rs, r_rs, s_ag, r_ag, s_kv, r_kv, s_dk, r_dk,
    s_rl, r_rl, s_fl, r_fl, s_os, r_os, s_oy, r_oy, s_oz, r_oz,
):
    row = lax.axis_index("row")
    col = lax.axis_index("col")
    x, z = lax.div(row, NZ), lax.rem(row, NZ)
    y, core = lax.div(col, 2), lax.rem(col, 2)
    head, quarter = lax.div(z, 4), lax.rem(z, 4)
    xs = [ring(x + d, NX) for d in range(NX)]
    zs = [ring(z + d, NZ) for d in range(NZ)]
    ys = [ring(y + d, NY) for d in range(NY)]
    sibling = col + 1 - 2 * core
    shift = 2 * core
    ls = [ring(z + shift + d, NZ) for d in range(NZ)]
    lz = ls[0]
    place_in_ring = 4 * x + lax.rem(lz, 4)

    def remote(src, dst, ssem, rsem, to_row, to_col):
        return pltpu.make_async_remote_copy(
            src_ref=src, dst_ref=dst, send_sem=ssem, recv_sem=rsem,
            device_id={"row": to_row, "col": to_col}, device_id_type=pl.DeviceIdType.MESH,
        )

    def token_row(i):
        at = lax.rem(place_in_ring + 16 + i, 16)
        return lax.div(at, 4) * NZ + ring(4 * lax.div(lz, 4) + lax.rem(at, 4) + NZ - shift, NZ)

    def x_row(side):
        return (xs[1] if side == 0 else xs[3]) * NZ + z

    def z_row(side):
        return x * NZ + (zs[1] if side == 0 else zs[7])

    barrier = pltpu.get_barrier_semaphore()

    def greet(to_row, to_col):
        pl.semaphore_signal(
            barrier, inc=1, device_id={"row": to_row, "col": to_col},
            device_id_type=pl.DeviceIdType.MESH,
        )

    at_home = core == head
    for j in range(4):
        @pl.when(4 * core + j != z)
        def _():
            greet(x * NZ + 4 * core + j, 2 * y + head)

    greet(z_row(0), col)
    greet(z_row(1), col)
    for d in range(1, NY):
        greet(row, 2 * ys[d] + core)
    for i in range(1, BACK + 1):
        greet(token_row(i), col)
        greet(token_row(-i), col)
    greet(row, sibling)
    greet(x_row(0), col)
    greet(x_row(1), col)

    def rows_at(i):
        return pl.ds(pl.multiple_of(PITCH * i, 16), SENT)

    own_rows = rows_at(x)
    for u in (KV, Q, OUT):
        w[u, pl.ds(pl.multiple_of(PITCH * x + 160, 16), 16), :] = jnp.zeros((16, 512), BF16)
    weight_rows = pl.ds(pl.multiple_of(PITCH * x, 16), OWN)
    for h in (0, 1):
        w[KV, weight_rows, 256 * h : 256 * h + 128] = wk_in[:, 128 * h : 128 * h + 128]
        w[KV, weight_rows, 256 * h + 128 : 256 * h + 256] = wv_in[:, 128 * h : 128 * h + 128]
    w[Q, weight_rows, :] = wq_in[...]
    w[OUT, weight_rows, :] = wo_in[...]

    for t, src in ((0, tok_in), (1, cot_in)):
        for j in range(4):
            piece[t, PITCH * j + 160 : PITCH * j + SENT] = jnp.zeros((SENT - 160, TOK), BF16)
            piece[t, PITCH * j : PITCH * j + OWN] = src[OWN * j : OWN * j + OWN]

    pl.semaphore_wait(barrier, 20 - at_home.astype(jnp.int32))

    def xf_copy(u, side, xx):
        slot = w.at[u, rows_at(xx)]
        return remote(slot, slot, s_xf.at[u, side], r_xf.at[u, side], x_row(side), col)

    def xh_copy(u, side, xx):
        slot = w.at[u, rows_at(xx), pl.ds(256 * side, 256)]
        return remote(slot, slot, s_xh.at[u, side], r_xh.at[u, side], x_row(side), col)

    def weight_start(u):
        xf_copy(u, 0, x).start()
        xf_copy(u, 1, x).start()

    def weight_forward(u):
        xf_copy(u, 0, xs[3]).wait_recv()
        xh_copy(u, 0, xs[3]).start()
        xf_copy(u, 1, xs[1]).wait_recv()
        xh_copy(u, 1, xs[1]).start()

    def weight_wait(u):
        xh_copy(u, 0, xs[2]).wait_recv()
        xh_copy(u, 1, xs[2]).wait_recv()

    def lanes_at(i):
        return pl.ds(pl.multiple_of(TOK * i, TOK), TOK)

    def half_at(c):
        return pl.ds(pl.multiple_of(512 * c, 512), 512)

    def piece_copy(t, j):
        return remote(
            piece.at[t, pl.ds(PITCH * j, SENT)], slabs.at[t, rows_at(y), lanes_at(z)],
            s_p.at[t, j], r_p.at[t, quarter], x * NZ + 4 * core + j, 2 * y + head,
        )

    def piece_recv(t, j):
        slot = slabs.at[t, rows_at(y), lanes_at(4 * core + j)]
        return remote(
            slot, slot, s_p.at[t, 0], r_p.at[t, j], x * NZ + 4 * core + j, 2 * y + head
        )

    def piece_start(t):
        for j in range(4):
            @pl.when(4 * core + j != z)
            def _():
                piece_copy(t, j).start()

            @pl.when(4 * core + j == z)
            def _():
                slabs[t, rows_at(y), lanes_at(z)] = piece[t, PITCH * j : PITCH * j + SENT]

    def slab_copy(t, dy, j, yy):
        slot = slabs.at[t, rows_at(yy), lanes_at(4 * core + j)]
        return remote(slot, slot, s_y.at[t, dy, j], r_y.at[t, dy, j], row, 2 * ys[dy] + core)

    def share_copy(t, dy, cc):
        slot = slabs.at[t, rows_at(ys[(NY - dy) % NY]), half_at(cc)]
        return remote(slot, slot, s_s.at[t, dy], r_s.at[t, dy], row, sibling)

    def collect(t):
        for i in range(4):
            j = lax.rem(quarter + i, 4)

            @pl.when(4 * core + j != z)
            def _():
                piece_recv(t, j).wait_recv()

            for dy in (1, 3, 2):
                slab_copy(t, dy, j, y).start()
        share_copy(t, 0, core).start()

    def share(t):
        for dy in (1, 3, 2):
            for j in range(4):
                slab_copy(t, dy, j, ys[NY - dy]).wait_recv()
            share_copy(t, dy, core).start()
        for dy in (0, 1, 3, 2):
            share_copy(t, dy, 1 - core).wait_recv()

    piece_start(0)
    weight_start(KV)
    weight_start(Q)
    piece_start(1)
    for j in range(4):
        gap = slice(PITCH * j + SENT, PITCH * (j + 1))
        for u in (KV, Q, OUT):
            w[u, gap, :] = jnp.zeros((PITCH - SENT, 512), BF16)
        for t in (0, 1):
            slabs[t, gap, :] = jnp.zeros((PITCH - SENT, SUPER), BF16)

    def lane_half(sub):
        return slice(HD * sub, HD * sub + HD)

    def rs_copy(u, sub, step, side):
        to = ls[5 - step] if side == 0 else ls[3 + step]
        return remote(
            part.at[u, to, :, pl.ds(HD * sub, HD)],
            sums.at[u, side, step - 1, :, pl.ds(HD * sub, HD)],
            s_rs.at[u, side, step - 1, sub], r_rs.at[u, side, step - 1, sub], z_row(side), col,
        )

    def rs_step(u, sub, n):
        lanes = lane_half(sub)
        for side in (sub, 1 - sub):
            step = n if side == sub else n + 1
            if step > 4:
                continue
            if n > 1:
                rs_copy(u, sub, step - 1, side).wait_recv()
                to = ls[5 - step] if side == 0 else ls[3 + step]
                part[u, to, :, lanes] = (
                    part[u, to, :, lanes].astype(F32) + sums[u, side, step - 2, :, lanes].astype(F32)
                ).astype(BF16)
            rs_copy(u, sub, step, side).start()

    def rs_both(u, n):
        rs_step(u, 0, n)
        rs_step(u, 1, n)

    def rs_total(u, sub):
        lanes = lane_half(sub)
        rs_copy(u, sub, 4, 1 - sub).wait_recv()
        rs_copy(u, sub, 4, sub).wait_recv()
        return (
            part[u, lz, :, lanes].astype(F32)
            + sums[u, 0, 3, :, lanes].astype(F32)
            + sums[u, 1, 3, :, lanes].astype(F32)
        ).astype(BF16)

    def ag_copy(v, sub, step, side, sending):
        back = step - 1 if sending else step
        slot = ls[(NZ - back) % NZ] if side == 0 else ls[back]
        block = gath.at[v, slot, :, pl.ds(HD * sub, HD)]
        return remote(
            block, block, s_ag.at[v, side, step - 1, sub], r_ag.at[v, side, step - 1, sub],
            z_row(side), col,
        )

    def ag_step(v, sub, n):
        for side in (sub, 1 - sub):
            steps = 4 if side == sub else 3
            if 1 <= n - 1 <= steps:
                ag_copy(v, sub, n - 1, side, False).wait_recv()
            if n <= steps:
                ag_copy(v, sub, n, side, True).start()

    def ag_both(v, n):
        ag_step(v, 0, n)
        ag_step(v, 1, n)

    def gathered(v, h):
        return gath[v, 4 * h : 4 * h + 4].reshape(SUPER, SLAB)

    def gathered_half(v, h, sub):
        return gath[v, 4 * h : 4 * h + 4, :, lane_half(sub)].reshape(SUPER, HD)

    def project(u, t):
        product = dot(slabs[t], w[u], 0, 0).astype(BF16)
        for h in (0, 1):
            part[u, 4 * h : 4 * h + 4] = product[:, 256 * h : 256 * h + 256].reshape(4, SLAB, SLAB)

    collect(0)
    weight_forward(KV)
    weight_forward(Q)
    weight_start(OUT)
    share(0)
    collect(1)
    weight_wait(KV)
    project(KV, 0)
    rs_both(KV, 1)
    weight_wait(Q)
    project(Q, 0)
    rs_both(KV, 2)
    rs_both(Q, 1)
    weight_forward(OUT)
    share(1)
    rs_both(KV, 3)
    rs_both(Q, 2)
    weight_wait(OUT)
    project(OUT, 1)
    rs_both(KV, 4)
    rs_both(Q, 3)
    rs_both(OUT, 1)
    own_keys = pl.ds(BACK * SLAB, SLAB)

    def kv_copy(i, sub):
        lanes = pl.ds(HD * sub, HD)
        return remote(
            kvwin.at[own_keys, lanes], kvwin.at[pl.ds((BACK - i) * SLAB, SLAB), lanes],
            s_kv.at[i - 1, sub], r_kv.at[i - 1, sub], token_row(i), col,
        )

    for sub in (0, 1):
        kvwin[own_keys, lane_half(sub)] = rs_total(KV, sub)
        for i in (3, 2, 1, 4):
            kv_copy(i, sub).start()
        if sub == 0:
            rs_both(Q, 4)

    def scale_of(values):
        return lax.rsqrt(jnp.mean(values * values, axis=-1, keepdims=True) + epsilon)

    qgain = qg_ref[...] * query_scalar ** (-0.5)
    kgain = kg_ref[...]

    def key_block(s):
        rows = slice(s * SLAB, s * SLAB + SLAB)
        k = kvwin[rows, 0:HD].astype(F32)
        kh[rows, :] = (k * scale_of(k) * kgain).astype(BF16)

    key_block(BACK)
    for r in range(2):
        q_raw[:, lane_half(r)] = rs_total(Q, r)
        q = q_raw[:, lane_half(r)].astype(F32)
        qh[SLAB * r : SLAB * r + SLAB, :] = (q * scale_of(q) * qgain).astype(BF16)

    def score_block(s):
        rows = slice(s * SLAB, s * SLAB + SLAB)
        scores[:, rows] = dot(qh[...], kh[rows, :], 1, 1)

    score_block(BACK)
    rs_both(OUT, 2)
    for i in (1, 4, 2, 3):
        kv_copy(i, 0).wait_recv()
        key_block(BACK - i)
        score_block(BACK - i)
    rs_both(OUT, 3)
    chunk = 64
    first_key = WINDOW - SLAB * place_in_ring

    def softmax(n):
        rows = pl.ds(pl.multiple_of(n * chunk, chunk), chunk)
        t0 = lax.rem(n, SLAB // chunk) * chunk
        t = t0 + lax.broadcasted_iota(jnp.int32, (chunk, 1), 0)
        key = lax.broadcasted_iota(jnp.int32, (chunk, KEYS), 1)
        allowed = (key <= t + WINDOW) & (key >= jnp.maximum(t + 1, first_key))
        s = jnp.where(allowed, scores[rows, :], -1e30)
        e = jnp.exp(s - jnp.max(s, axis=-1, keepdims=True))
        pb[rows, :] = (e * (1.0 / jnp.sum(e, axis=-1, keepdims=True))).astype(BF16)

    pl.loop(0, SLAB // chunk)(softmax)
    rs_both(OUT, 4)
    pl.loop(SLAB // chunk, 2 * SLAB // chunk)(softmax)
    for i in range(1, BACK + 1):
        kv_copy(i, 1).wait_recv()

    def dk_copy(i, sub):
        lanes = pl.ds(HD * sub, HD)
        return remote(
            dkv.at[BACK - i, :, lanes], dkv_in.at[i - 1, :, lanes],
            s_dk.at[i - 1, sub], r_dk.at[i - 1, sub], token_row(-i), col,
        )

    def owned(sub):
        for i in range(1, BACK + 1):
            dk_copy(i, sub).wait_recv()
        total = dkv_own[:, lane_half(sub)]
        for i in range(BACK):
            total = total + dkv_in[i, :, lane_half(sub)].astype(F32)
        gath[DKV, lz, :, lane_half(sub)] = total.astype(BF16)

    blended = dot(pb[...], kvwin[:, HD:], 1, 0).astype(BF16)
    for r in range(2):
        gath[ATT, lz, :, lane_half(r)] = blended[SLAB * r : SLAB * r + SLAB]
    ag_both(ATT, 1)
    for r in range(2):
        datt[SLAB * r : SLAB * r + SLAB, :] = rs_total(OUT, r)
    dvh = dot(pb[...], datt[...], 0, 0)
    dkv_own[:, HD:] = dvh[BACK * SLAB :]
    for s in range(BACK):
        dkv[s, :, HD:] = dvh[s * SLAB : s * SLAB + SLAB].astype(BF16)
    for i in (3, 2, 1, 4):
        dk_copy(i, 1).start()

    scores[...] = dot(datt[...], kvwin[:, HD:], 1, 1)

    def softmax_back(n):
        rows = pl.ds(pl.multiple_of(n * chunk, chunk), chunk)
        p = pb[rows, :].astype(F32)
        dp = scores[rows, :]
        delta = jnp.sum(p * dp, axis=-1, keepdims=True)
        ds[rows, :] = (p * (dp - delta)).astype(BF16)

    pl.loop(0, SLAB // chunk)(softmax_back)
    ag_both(ATT, 2)
    pl.loop(SLAB // chunk, 2 * SLAB // chunk)(softmax_back)

    def norm_back(raw, gain, grad):
        r = scale_of(raw)
        inner = grad * gain
        return r * inner - raw * (r * r * r * jnp.mean(raw * inner, axis=-1, keepdims=True))

    dkh = dot(ds[...], qh[...], 0, 0)
    for s in range(BACK + 1):
        rows = slice(s * SLAB, s * SLAB + SLAB)
        dk = norm_back(kvwin[rows, 0:HD].astype(F32), kgain, dkh[rows])
        if s == BACK:
            dkv_own[:, 0:HD] = dk
        else:
            dkv[s, :, 0:HD] = dk.astype(BF16)
    for i in (3, 2, 1, 4):
        dk_copy(i, 0).start()
    owned(1)
    ag_step(DKV, 1, 1)

    dqh = dot(ds[...], kh[...], 1, 0)
    for r in range(2):
        gath[DQ, lz, :, lane_half(r)] = norm_back(
            q_raw[:, lane_half(r)].astype(F32), qgain, dqh[SLAB * r : SLAB * r + SLAB]
        ).astype(BF16)
    ag_both(DQ, 1)
    ag_both(ATT, 3)
    ag_step(DKV, 1, 2)

    def rl_copy(u, side):
        return remote(
            g.at[u, rows_at(xs[2]), pl.ds(256 * side, 256)], relay.at[u, side],
            s_rl.at[u, side], r_rl.at[u, side], x_row(side), col,
        )

    def fl_copy(u, side):
        return remote(
            g.at[u, rows_at(xs[1] if side == 0 else xs[3])], full.at[u, side],
            s_fl.at[u, side], r_fl.at[u, side], x_row(side), col,
        )

    def grad_start(u, t, v):
        for h in (0, 1):
            g[u, :, 256 * h : 256 * h + 256] = dot(slabs[t], gathered(v, h), 1, 0).astype(BF16)
        rl_copy(u, 0).start()
        rl_copy(u, 1).start()

    def grad_middle(u):
        for side in (0, 1):
            rl_copy(u, side).wait_recv()
            rows = rows_at(xs[1] if side == 0 else xs[3])
            lanes = slice(256 * side, 256 * side + 256)
            g[u, rows, lanes] = (
                g[u, rows, lanes].astype(F32) + relay[u, side].astype(F32)
            ).astype(BF16)
            fl_copy(u, side).start()

    def grad_last(u):
        fl_copy(u, 0).wait_recv()
        fl_copy(u, 1).wait_recv()
        total = (
            g[u, own_rows, :].astype(F32)
            + full[u, 0].astype(F32)
            + full[u, 1].astype(F32)
        ).astype(BF16)
        return total[0:OWN]

    def os_copy(t, dy, cc):
        return remote(
            ypart.at[t, rows_at(ys[dy]), half_at(1 - cc)], ysib.at[t, dy],
            s_os.at[t, dy], r_os.at[t, dy], row, sibling,
        )

    def oy_copy(t, dy, j):
        return remote(
            ypart.at[t, rows_at(ys[dy]), lanes_at(4 * core + j)],
            yrecv.at[t, dy - 1, :, pl.ds(TOK * j, TOK)],
            s_oy.at[t, dy, j], r_oy.at[t, dy, j], row, 2 * ys[dy] + core,
        )

    def oz_copy(t, j):
        return remote(
            ypart.at[t, rows_at(y), lanes_at(4 * core + j)], last.at[t, rows_at(quarter)],
            s_oz.at[t, j], r_oz.at[t, quarter], x * NZ + 4 * core + j, 2 * y + head,
        )

    def oz_recv(t, j):
        slot = last.at[t, pl.ds(PITCH * j, SENT)]
        return remote(
            slot, slot, s_oz.at[t, j], r_oz.at[t, j], x * NZ + 4 * core + j, 2 * y + head
        )

    def out_start(t):
        for dy in (2, 1, 3, 0):
            os_copy(t, dy, core).start()

    def out_middle(t):
        for dy in (2, 1, 3, 0):
            os_copy(t, dy, core).wait_recv()
            rows, lanes = rows_at(ys[dy]), half_at(core)
            ypart[t, rows, lanes] = (
                ypart[t, rows, lanes].astype(F32) + ysib[t, dy].astype(F32)
            ).astype(BF16)
            if dy == 2:
                for j in range(4):
                    oy_copy(t, 2, j).start()
            if dy == 3:
                for j in range(4):
                    oy_copy(t, 1, j).start()
                    oy_copy(t, 3, j).start()

    def out_sum(t):
        rows = rows_at(y)
        for j in range(4):
            lanes = lanes_at(4 * core + j)
            total = ypart[t, rows, lanes].astype(F32)
            for dy in (2, 1, 3):
                oy_copy(t, dy, j).wait_recv()
                total = total + yrecv[t, dy - 1, :, TOK * j : TOK * j + TOK].astype(F32)
            ypart[t, rows, lanes] = total.astype(BF16)

            @pl.when(4 * core + j != z)
            def _():
                oz_copy(t, j).start()

            @pl.when(4 * core + j == z)
            def _():
                last[t, PITCH * j : PITCH * j + SENT] = total.astype(BF16)

    def out_last(t, out):
        for j in range(4):
            @pl.when(4 * core + j != z)
            def _():
                oz_recv(t, j).wait_recv()
        for j in range(4):
            out[OWN * j : OWN * j + OWN] = last[t, PITCH * j : PITCH * j + OWN]

    owned(0)
    ag_step(DKV, 0, 1)
    ag_both(ATT, 4)
    ag_both(DQ, 2)
    ag_step(DKV, 0, 2)
    ag_step(DKV, 1, 3)
    ag_both(ATT, 5)
    grad_start(OUT, 1, ATT)
    ag_step(DKV, 0, 3)
    ag_both(DQ, 3)
    ag_step(DKV, 1, 4)
    ypart[0] = (
        dot(w[OUT, :, 0:256], gathered(ATT, 0), 1, 1)
        + dot(w[OUT, :, 256:512], gathered(ATT, 1), 1, 1)
    ).astype(BF16)
    out_start(0)
    ag_step(DKV, 0, 4)
    ag_both(DQ, 4)
    grad_middle(OUT)
    out_middle(0)
    ag_step(DKV, 1, 5)
    ag_both(DQ, 5)
    rest[...] = (
        dot(w[Q, :, 0:256], gathered(DQ, 0), 1, 1)
        + dot(w[Q, :, 256:512], gathered(DQ, 1), 1, 1)
        + dot(w[KV, :, 128:256], gathered_half(DKV, 0, 1), 1, 1)
        + dot(w[KV, :, 384:512], gathered_half(DKV, 1, 1), 1, 1)
    )
    grad_start(Q, 0, DQ)
    ag_step(DKV, 0, 5)
    for dy in (2, 1, 3, 0):
        rows = pl.ds(pl.multiple_of(PITCH * ys[dy], 16), PITCH)
        ypart[1, rows, :] = (
            rest[rows, :]
            + dot(w[KV, rows, 0:128], gathered_half(DKV, 0, 0), 1, 1)
            + dot(w[KV, rows, 256:384], gathered_half(DKV, 1, 0), 1, 1)
        ).astype(BF16)
        os_copy(1, dy, core).start()
    out_middle(1)
    grad_start(KV, 0, DKV)
    grad_middle(Q)
    grad_middle(KV)
    out_sum(0)
    go_out[...] = grad_last(OUT)
    out_sum(1)
    gq_out[...] = grad_last(Q)
    done = grad_last(KV)
    for h in (0, 1):
        gk_out[:, 128 * h : 128 * h + 128] = done[:, 256 * h : 256 * h + 128]
        gv_out[:, 128 * h : 128 * h + 128] = done[:, 256 * h + 128 : 256 * h + 256]
    out_last(0, layer_out)
    out_last(1, input_grad)

    for u in (KV, Q, OUT):
        for side in (0, 1):
            xf_copy(u, side, x).wait_send()
            xh_copy(u, side, xs[3] if side == 0 else xs[1]).wait_send()
            rl_copy(u, side).wait_send()
            fl_copy(u, side).wait_send()
            for sub in (0, 1):
                for step in range(1, 5):
                    if step > 1 or side == sub:
                        rs_copy(u, sub, step, side).wait_send()
                    if step < 4 or side == sub:
                        ag_copy(u, sub, step, side, True).wait_send()
    for t in (0, 1):
        for j in range(4):
            @pl.when(4 * core + j != z)
            def _():
                piece_copy(t, j).wait_send()
                oz_copy(t, j).wait_send()
        for dy in range(NY):
            share_copy(t, dy, core).wait_send()
            os_copy(t, dy, core).wait_send()
            if dy:
                for j in range(4):
                    slab_copy(t, dy, j, y).wait_send()
                    oy_copy(t, dy, j).wait_send()

    for i in range(1, BACK + 1):
        for sub in (0, 1):
            kv_copy(i, sub).wait_send()
            dk_copy(i, sub).wait_send()


def hand_over(*refs):
    for source, target in zip(refs[:6], refs[6:]):
        target[...] = source[...]


def shards(tokens, w_query, w_key, w_value, w_output, query_gain, key_gain, cotangent):
    vmem = lambda *shape, dtype=BF16: pltpu.VMEM(shape, dtype)
    dma = lambda *shape: pltpu.SemaphoreType.DMA(shape)
    spec = pl.BlockSpec(memory_space=pltpu.VMEM)
    scratch = [
        vmem(2, BLOCK, TOK), vmem(2, BLOCK, SUPER),
        vmem(3, BLOCK, 512), vmem(3, BLOCK, 512),
        vmem(3, NZ, SLAB, SLAB), vmem(3, 2, 4, SLAB, SLAB),
        vmem(3, NZ, SLAB, SLAB),
        vmem(SLAB, SLAB), vmem(2 * SLAB, HD), vmem(KEYS, HD), vmem(KEYS, 2 * HD),
        vmem(2 * SLAB, KEYS, dtype=F32), vmem(2 * SLAB, KEYS), vmem(2 * SLAB, KEYS),
        vmem(2 * SLAB, HD),
        vmem(BACK, SLAB, 256), vmem(SLAB, 256, dtype=F32), vmem(BACK, SLAB, 256),
        vmem(2, BLOCK, SUPER), vmem(BLOCK, SUPER, dtype=F32),
        vmem(2, NY, SENT, 512), vmem(2, 3, SENT, 512),
        vmem(2, BLOCK, TOK), vmem(3, 2, SENT, 256), vmem(3, 2, SENT, 512),
        dma(3, 2), dma(3, 2), dma(3, 2), dma(3, 2),
        dma(2, 4), dma(2, 4), dma(2, NY, 4), dma(2, NY, 4), dma(2, NY), dma(2, NY),
        dma(3, 2, 4, 2), dma(3, 2, 4, 2), dma(3, 2, 4, 2), dma(3, 2, 4, 2),
        dma(BACK, 2), dma(BACK, 2), dma(BACK, 2), dma(BACK, 2),
        dma(3, 2), dma(3, 2), dma(3, 2), dma(3, 2),
        dma(2, NY), dma(2, NY), dma(2, NY, 4), dma(2, NY, 4), dma(2, 4), dma(2, 4),
    ]
    outs = [
        jax.ShapeDtypeStruct(tokens.shape[::-1], BF16),
        jax.ShapeDtypeStruct(tokens.shape[::-1], BF16),
        jax.ShapeDtypeStruct(w_query.shape, BF16),
        jax.ShapeDtypeStruct(w_key.shape, BF16),
        jax.ShapeDtypeStruct(w_value.shape, BF16),
        jax.ShapeDtypeStruct(w_output.shape[::-1], BF16),
    ]
    results = pl.pallas_call(
        kernel,
        out_shape=outs,
        in_specs=[spec] * 8,
        out_specs=[spec] * 6,
        scratch_shapes=scratch,
        compiler_params=pltpu.CompilerParams(
            collective_id=0, has_side_effects=True, vmem_limit_bytes=60 * 1024 * 1024
        ),
    )(
        tokens.T, cotangent.T, w_query, w_key, w_value, w_output.T,
        query_gain.reshape(1, HD), key_gain.reshape(1, HD),
    )
    layer_out, input_grad, gq, gk, gv, go = pl.pallas_call(
        hand_over, out_shape=outs, in_specs=[spec] * 6, out_specs=[spec] * 6
    )(*results)
    return layer_out.T, input_grad.T, gq, gk, gv, go.T


def solution(mesh):
    in_specs = (
        P("row", "col"), P("row", "col"), P("row", "col"), P("row", "col"), P("col", "row"),
        P(), P(), P("row", "col"),
    )
    out_specs = (
        P("row", "col"), P("row", "col"), P("row", "col"), P("row", "col"), P("row", "col"),
        P("col", "row"),
    )
    return jax.shard_map(shards, mesh=mesh, in_specs=in_specs, out_specs=out_specs, check_vma=False)
```
